512 devices in a mesh: row: 64 (over z, y), col: 8 (over x, core).
Axes of the slice: x: 4, y: 8, z: 8, core: 2. Of those that a mesh axis runs over, the one named last changes fastest.
Arguments:
- pool: float32 [131072, 128], P('row'), may hold values from -6 to 6
- window_index: int32 [16384], P('row'), may hold values from 0 to 2047
- pool_labels: int32 [131072], P('row'), may hold values from 0 to 9
- val_embed: float32 [32768, 128], P('col', 'row'), may hold values from -6 to 6
- val_labels: int32 [32768], P('col'), may hold values from 0 to 9
- class_cost: float32 [10, 10], replicated, may hold values from 0 to 1
Outputs:
- value: float32 [16384], P('row')
- potential_val: float32 [32768], P('col')
The draws below stay inside these ranges and needn't reach their ends.
Inputs may be any that keep to these rules, and one draw needn't show every extreme that they name: `window_index`: window example i reads pool row (i // 256) * 2048 + window_index_i.
All inputs are finite; a program needn't handle non-finite values.
Results may differ from the reference program's by a relative error of at most 0.0003.
Values sent between devices are 32-bit elements; how exact they have to be, the bound alone decides.
No kernel may reach another device: no remote copies, remote signals or barrier semaphores. Data moves between devices by JAX's collectives and lax.ppermute only.
A program may use at most 64 MiB of HBM per device.

```python
import math
import jax
import jax.numpy as jnp
from jax import lax

DIM = 128
CLASSES = 10
ITERS = 2
TR_DEV = 256
POOL_DEV = 2048
TRAIN = 16384
VAL = 32768
POOL = 131072


def plant(entries, stream_key, least, high):
    place = [jax.random.randint(jax.random.fold_in(stream_key, axis), (), 0, length) for axis, length in enumerate(entries.shape)]
    main_axis = entries.shape.index(max(entries.shape))
    beside = place[:main_axis] + [(place[main_axis] + 1) % entries.shape[main_axis]] + place[main_axis + 1:]
    return entries.at[tuple(place)].set(least).at[tuple(beside)].set(high)


def levels(own_key, extent, shards, low, top_value):
    loudness, own = 1.0, jax.random.fold_in(own_key, 6)
    for axis_at, parts in shards:
        draws = jnp.exp(jax.random.uniform(jax.random.fold_in(own, axis_at), (parts,), jnp.float32, low / len(shards), top_value / len(shards)))
        loudness = loudness * jnp.repeat(draws, extent[axis_at] // parts).reshape([-1 if axis == axis_at else 1 for axis in range(len(extent))])
    return loudness


def scatter_about(rng, shape, spread, bound, split=(), kind=jnp.bfloat16):
    gain = levels(rng, shape, split, -0.22, 0.18) if split else 1.0
    array = jax.random.normal(rng, shape, jnp.float32) * spread * gain
    return jnp.minimum(jnp.maximum(array, -bound), bound).astype(kind)


def setup_inputs(seed: int = 0) -> dict:
    key_of = jax.random.split(jax.random.key(seed), 7)
    return {
        "pool": scatter_about(key_of[0], (POOL, DIM), 1.0, 6.0, ((0, 64),), jnp.float32),
        "window_index": plant(jax.random.randint(key_of[1], (TRAIN,), 0, POOL_DEV), jax.random.fold_in(key_of[1], 1), 0, POOL_DEV - 1).astype(jnp.int32),
        "pool_labels": plant(jax.random.randint(key_of[2], (POOL,), 0, CLASSES), jax.random.fold_in(key_of[2], 1), 0, CLASSES - 1).astype(jnp.int32),
        "val_embed": scatter_about(key_of[3], (VAL, DIM), 1.0, 6.0, ((0, 8), (1, 64)), jnp.float32),
        "val_labels": plant(jax.random.randint(key_of[4], (VAL,), 0, CLASSES), jax.random.fold_in(key_of[4], 1), 0, CLASSES - 1).astype(jnp.int32),
        "class_cost": jnp.clip(jax.random.uniform(key_of[5], (CLASSES, CLASSES), jnp.float32, 0.0, 1.0), 0.0, 1.0),
    }


EPSILON = 0.02


def cost_rows(rows, row_labels, val_t, val_onehot_t, class_cost):
    squares_r = jnp.sum(rows * rows, axis=1)
    squares_v = jnp.sum(val_t * val_t, axis=0)
    cross = jnp.dot(rows, val_t, precision=lax.Precision.HIGHEST, preferred_element_type=jnp.float32)
    onehot = (row_labels[:, None] == jnp.arange(class_cost.shape[0], dtype=jnp.int32)[None, :]).astype(jnp.float32)
    mapped = jnp.dot(onehot, class_cost, precision=lax.Precision.HIGHEST, preferred_element_type=jnp.float32)
    label = jnp.dot(mapped, val_onehot_t, precision=lax.Precision.HIGHEST, preferred_element_type=jnp.float32)
    return (squares_r[:, None] + squares_v[None, :] - 2.0 * cross) / rows.shape[1] + label


def reference(pool, window_index, pool_labels, val_embed, val_labels, class_cost):
    total = window_index.shape[0]
    count = val_labels.shape[0]
    where = (jnp.arange(total, dtype=jnp.int32) // TR_DEV) * POOL_DEV + window_index.astype(jnp.int32)
    rows = pool[where]
    row_labels = pool_labels[where]
    val_t = val_embed.T
    val_onehot_t = (jnp.arange(CLASSES, dtype=jnp.int32)[:, None] == val_labels[None, :]).astype(jnp.float32)
    nblocks = total // TR_DEV
    row_blocks = rows.reshape(nblocks, TR_DEV, rows.shape[1])
    label_blocks = row_labels.reshape(nblocks, TR_DEV)
    log_a = -math.log(total)
    log_b = -math.log(count)
    potential_val = jnp.zeros((count,), jnp.float32)
    for step in range(ITERS):
        def row_update(pair):
            tile = cost_rows(pair[0], pair[1], val_t, val_onehot_t, class_cost)
            z = (potential_val[None, :] - tile) / EPSILON
            top = jnp.max(z, axis=1)
            return EPSILON * log_a - EPSILON * (top + jnp.log(jnp.sum(jnp.exp(z - top[:, None]), axis=1)))

        f = lax.map(row_update, (row_blocks, label_blocks)).reshape(total)
        f_blocks = f.reshape(nblocks, TR_DEV)

        def col_update(carry, item):
            tile = cost_rows(item[0], item[1], val_t, val_onehot_t, class_cost)
            z = (item[2][:, None] - tile) / EPSILON
            newtop = jnp.maximum(carry[0], jnp.max(z, axis=0))
            total_exp = carry[1] * jnp.exp(carry[0] - newtop) + jnp.sum(jnp.exp(z - newtop[None, :]), axis=0)
            return (newtop, total_exp), None

        start = (jnp.full((count,), -jnp.inf, jnp.float32), jnp.zeros((count,), jnp.float32))
        (top, total_exp), unused = lax.scan(col_update, start, (row_blocks, label_blocks, f_blocks))
        potential_val = EPSILON * log_b - EPSILON * (top + jnp.log(total_exp))
    value = f - jnp.sum(f) / total
    return value, potential_val
```

```python
import math

import jax
import jax.numpy as jnp
from jax import lax
from jax.experimental import pallas as pl
from jax.experimental.pallas import tpu as pltpu
from jax.sharding import Mesh
from jax.sharding import PartitionSpec as P

EPSILON = 0.02
SCALE = 1.0 / (EPSILON * math.log(2.0))
BACK = EPSILON * math.log(2.0)

ROW = ("z2", "z1", "z0", "y2", "y1", "y0")
COL = ("x", "core")
QUAD = ("z0", "y0")
ACROSS = ("z2", "z1", "y2", "y1")
ALONG = QUAD + COL

T = 128
NB = 8
SIDE = NB * T
PARAMS = pltpu.CompilerParams(vmem_limit_bytes=48 * 1024 * 1024)
F32 = jnp.float32
BF16 = jnp.bfloat16


def split3(x):
    hi = x.astype(BF16)
    rest = x - hi.astype(F32)
    mid = rest.astype(BF16)
    low = (rest - mid.astype(F32)).astype(BF16)
    return hi, mid, low


def lse_lead(parts):
    top = jnp.max(parts, axis=0)
    return top + jnp.log2(jnp.sum(jnp.exp2(parts - top[None]), axis=0))


def lse_list(zs):
    top = zs[0]
    for z in zs[1:]:
        top = jnp.maximum(top, z)
    total = jnp.exp2(zs[0] - top)
    for z in zs[1:]:
        total = total + jnp.exp2(z - top)
    return top, total


def columns_kernel(val_ref, out_ref):
    for quarter in range(4):
        for block in range(NB):
            piece = val_ref[:, pl.ds((quarter * NB + block) * T, T)]
            for feature in range(2):
                row = piece[feature : feature + 1]
                for z in range(4):
                    for y in range(4):
                        target = ((z * 2 + quarter // 2) * 4 + y) * 2 + quarter % 2
                        out_ref[target, pl.ds(feature * NB + block, 1), :] = row


def rows_kernel(index_ref, labels_ref, pool_ref, out_ref, column_ref):
    count = index_ref.shape[0]

    def step(i, carry):
        for j in range(8):
            at = i * 8 + j
            place = index_ref[at]
            out_ref[0, pl.ds(at, 1), :] = pool_ref[pl.ds(place, 1), :]
            column_ref[pl.ds(at, 1), :] = jnp.full((1, T), labels_ref[place].astype(F32), F32)
        return carry

    lax.fori_loop(0, count // 8, step, 0)
    out_ref[0, count : count + 8, :] = jnp.zeros((8, T), F32)
    for k in range(count // T):
        flat = column_ref[k * T : (k + 1) * T, :].T
        out_ref[0, count + k : count + k + 1, :] = flat[0:1]
    for copy in range(1, 4):
        out_ref[copy] = out_ref[0]


def row_lse(load, at_ref, out_ref):
    def block_step(s, carry):
        for piece in range(T // 32):
            rows = pl.ds(s * T + piece * 32, 32)
            top, total = lse_list([load(block, rows) for block in range(NB)])
            at_ref[piece * 32 : (piece + 1) * 32, :] = top + jnp.log2(total)
        flat = at_ref[...].T
        top = jnp.max(flat, axis=0, keepdims=True)
        lse = top + jnp.log2(jnp.sum(jnp.exp2(flat - top), axis=0, keepdims=True))
        out_ref[pl.ds(s, 1), :] = lse
        return carry

    lax.fori_loop(0, NB, block_step, 0)


def cost_kernel(rows_ref, val_ref, quarter_ref, labels_ref, class_ref, cost_ref, out_ref, b_ref, sq_ref, at_ref, part_ref):
    count = 256
    classes = class_ref.shape[0]
    own = labels_ref[pl.ds(pl.multiple_of(quarter_ref[0] * NB, NB), NB), :]
    kinds = class_ref[...] * (-SCALE)
    for block in range(NB):
        lanes = slice(block * T, (block + 1) * T)
        y = val_ref[pl.ds(block, T, stride=NB), :]
        hi, mid, low = split3(y)
        for k, part in enumerate((hi, mid, hi, low, hi, mid)):
            b_ref[k * T : (k + 1) * T, lanes] = part
        sq_ref[0:1, lanes] = jnp.sum(y * y, axis=0, keepdims=True) * (-SCALE / T)
        onehot = (lax.broadcasted_iota(jnp.int32, (classes, T), 0) == own[block : block + 1]).astype(F32)
        mapped = jnp.dot(kinds, onehot, precision=lax.Precision.HIGHEST, preferred_element_type=F32)
        mapped = jnp.concatenate([mapped, jnp.zeros((16 - classes, T), F32)], axis=0)
        hi, mid, low = split3(mapped)
        b_ref[6 * T : 7 * T, lanes] = jnp.concatenate([hi, mid, low, jnp.zeros((T - 48, T), BF16)], axis=0)
    for group in range(4):
        x = rows_ref[group, 0:count, :]
        squares = jnp.sum(x * x, axis=1, keepdims=True) * (-SCALE / T)
        hi, mid, low = split3(x * (2.0 * SCALE / T))
        lane = lax.broadcasted_iota(jnp.int32, (count, T), 1)
        flat = [
            jnp.broadcast_to(rows_ref[group, count + k : count + k + 1, :], (T, T)).T for k in range(count // T)
        ]
        label = jnp.concatenate(flat, axis=0).astype(jnp.int32)
        ext = jnp.where((lane % 16 == label) & (lane < 48), 1.0, 0.0).astype(BF16)
        a = jnp.concatenate([hi, hi, mid, hi, low, mid, ext], axis=1)
        product = jnp.dot(a, b_ref[...], preferred_element_type=F32)
        cost_ref[group * count : (group + 1) * count, :] = product + squares + sq_ref[0:1, :]
    row_lse(lambda block, rows: cost_ref[rows, block * T : (block + 1) * T], at_ref, part_ref)
    for k in range(out_ref.shape[0]):
        out_ref[k] = part_ref[...]


def rows_step_kernel(parts_ref, cost_ref, out_ref, at_ref, part_ref):
    g = -15.0 - lse_lead(parts_ref[...])
    wide = [jnp.broadcast_to(g[block : block + 1], (32, T)) for block in range(NB)]
    row_lse(lambda block, rows: cost_ref[rows, block * T : (block + 1) * T] + wide[block], at_ref, part_ref)
    for k in range(out_ref.shape[0]):
        out_ref[k] = part_ref[...]


def column_lse(f, cost_ref, wide_ref, part_ref):
    for s in range(NB):
        wide_ref[s * T : (s + 1) * T, :] = jnp.broadcast_to(f[s : s + 1], (T, T)).T
    for block in range(NB):
        lanes = slice(block * T, (block + 1) * T)

        def chunk(k, carry):
            start = pl.multiple_of(k * 64, 64)
            zs = [
                cost_ref[pl.ds(start + 8 * j, 8), lanes] + wide_ref[pl.ds(start + 8 * j, 8), :]
                for j in range(8)
            ]
            top, total = lse_list(zs)
            newtop = jnp.maximum(carry[0], top)
            return newtop, carry[1] * jnp.exp2(carry[0] - newtop) + total * jnp.exp2(top - newtop)

        start = (jnp.full((8, T), -3.0e38, F32), jnp.zeros((8, T), F32))
        top, total = lax.fori_loop(0, SIDE // 64, chunk, start, unroll=4)
        best = jnp.max(top, axis=0, keepdims=True)
        whole = jnp.sum(total * jnp.exp2(top - best), axis=0, keepdims=True)
        part_ref[block : block + 1, :] = best + jnp.log2(whole)


def columns_step_kernel(parts_ref, cost_ref, out_ref, wide_ref, part_ref):
    f = -14.0 - lse_lead(parts_ref[...])
    column_lse(f, cost_ref, wide_ref, part_ref)
    for k in range(out_ref.shape[0]):
        out_ref[k] = part_ref[...]


def last_columns_kernel(parts_ref, cost_ref, out_ref, f_ref, wide_ref, part_ref):
    f = -14.0 - lse_lead(parts_ref[...])
    f_ref[...] = f
    column_lse(f, cost_ref, wide_ref, part_ref)
    total = jnp.broadcast_to(jnp.sum(f, axis=0, keepdims=True), (NB, T))
    for k in range(out_ref.shape[0]):
        out_ref[k, 0:NB, :] = part_ref[...]
        out_ref[k, NB : 2 * NB, :] = total


def finish_kernel(parts_ref, f_ref, quarter_ref, value_ref, potential_ref):
    total = jnp.zeros((NB, T), F32)
    for k in range(parts_ref.shape[0]):
        total = total + parts_ref[k, NB : 2 * NB, :]
    mean = jnp.sum(total[0:1]) * (0.25 / 16384.0)
    value_ref[...] = (f_ref[pl.ds(quarter_ref[0] * 2, 2), :] - mean) * BACK
    for quarter in range(4):
        parts = [
            parts_ref[((z * 2 + quarter // 2) * 4 + y) * 2 + quarter % 2, 0:NB, :] for z in range(4) for y in range(4)
        ]
        top, whole = lse_list(parts)
        potential_ref[quarter * NB : (quarter + 1) * NB, :] = (-15.0 - (top + jnp.log2(whole))) * BACK


def vmem(shape, dtype=F32):
    return pltpu.VMEM(shape, dtype)


SPEC = pl.BlockSpec(memory_space=pltpu.VMEM)
SCALARS = pl.BlockSpec(memory_space=pltpu.SMEM)


def call(kernel, out, ins, scratch=()):
    def shape(s):
        return jax.ShapeDtypeStruct(s, F32)

    return pl.pallas_call(
        kernel,
        out_shape=[shape(s) for s in out],
        in_specs=[SCALARS if i else SPEC for i in ins],
        out_specs=[SPEC] * len(out),
        scratch_shapes=list(scratch),
        compiler_params=PARAMS,
    )


def local(pool, window_index, pool_labels, val_embed, val_labels, class_cost):
    quarter = lax.axis_index(QUAD).astype(jnp.int32).reshape(1)
    (columns,) = call(columns_kernel, [(64, 16, T)], [0])(val_embed.T)
    (rows,) = call(rows_kernel, [(4, 264, T)], [1, 1, 0], [vmem((256, T))])(window_index, pool_labels, pool)
    columns = lax.all_to_all(columns, ROW, 0, 0)
    rows = lax.all_to_all(rows, QUAD, 0, 0)
    flat, wide = vmem((T, T)), vmem((SIDE, T))
    part = vmem((NB, T))
    cost, parts = call(
        cost_kernel,
        [(SIDE, SIDE), (32, NB, T)],
        [0, 0, 1, 0, 0],
        [vmem((7 * T, SIDE), BF16), vmem((8, SIDE)), flat, part],
    )(rows, columns.reshape(SIDE, T), quarter, val_labels.reshape(32, T), class_cost)
    parts = lax.all_to_all(parts, ALONG, 0, 0)
    (parts,) = call(columns_step_kernel, [(16, NB, T)], [0, 0], [wide, part])(parts, cost)
    parts = lax.all_to_all(parts, ACROSS, 0, 0)
    (parts,) = call(rows_step_kernel, [(32, NB, T)], [0, 0], [flat, part])(parts, cost)
    parts = lax.all_to_all(parts, ALONG, 0, 0)
    parts, f = call(last_columns_kernel, [(64, 2 * NB, T), (NB, T)], [0, 0], [wide, part])(parts, cost)
    parts = lax.all_to_all(parts, ROW, 0, 0)
    value, potential = call(finish_kernel, [(2, T), (32, T)], [0, 0, 1])(parts, f, quarter)
    return value.reshape(256), potential.reshape(4096)


def solution(mesh):
    fine = Mesh(mesh.devices.reshape(2, 2, 2, 2, 2, 2, 4, 2), ROW + COL)
    placed = (P(ROW, None), P(ROW), P(ROW), P(COL, ROW), P(COL), P())
    return jax.shard_map(local, mesh=fine, in_specs=placed, out_specs=(P(ROW), P(COL)), check_vma=False)
```

```python
import math

import jax
import jax.numpy as jnp
from jax import lax
from jax.experimental import pallas as pl
from jax.experimental.pallas import tpu as pltpu
from jax.sharding import Mesh
from jax.sharding import PartitionSpec as P

EPSILON = 0.02
SCALE = 1.0 / (EPSILON * math.log(2.0))
BACK = EPSILON * math.log(2.0)

ROW = ("z2", "z1", "z0", "y2", "y1", "y0")
COL = ("x", "core")
QUAD = ("z0", "y0")
ACROSS = ("z2", "z1", "y2", "y1")
ALONG = QUAD + COL

T = 128
NB = 8
SIDE = NB * T
OWN = 256
PARAMS = pltpu.CompilerParams(vmem_limit_bytes=20 * 1024 * 1024)
F32 = jnp.float32
BF16 = jnp.bfloat16


def split3(x):
    hi = x.astype(BF16)
    rest = x - hi.astype(F32)
    mid = rest.astype(BF16)
    low = (rest - mid.astype(F32)).astype(BF16)
    return hi, mid, low


def member(quarter, z, y):
    return ((z * 2 + quarter // 2) * 4 + y) * 2 + quarter % 2


def tree(op, xs):
    xs = list(xs)
    while len(xs) > 1:
        xs = [op(*xs[i : i + 2]) if i + 1 < len(xs) else xs[i] for i in range(0, len(xs), 2)]
    return xs[0]


def lse_list(zs):
    top = tree(jnp.maximum, zs)
    return top, tree(jnp.add, [jnp.exp2(z - top) for z in zs])


def lse_lead(parts_ref):
    top, total = lse_list([parts_ref[k] for k in range(parts_ref.shape[0])])
    return top + jnp.log2(total)


def send(part_ref, out_ref):
    part = part_ref[...]
    for k in range(out_ref.shape[0]):
        out_ref[k] = part


def prepare_kernel(
    index_hbm, labels_hbm, pool_hbm, val_hbm, columns_ref, rows_ref, index_ref, labels_ref, pool_ref, val_ref, column_ref, sems
):
    moves = [(val_hbm, val_ref), (index_hbm, index_ref), (labels_hbm, labels_ref), (pool_hbm, pool_ref)]
    copies = [pltpu.make_async_copy(a, b, sems.at[k]) for k, (a, b) in enumerate(moves)]
    for copy in copies:
        copy.start()
    copies[0].wait()
    for quarter in range(4):
        first = member(quarter, 0, 0)
        for block in range(NB):
            piece = val_ref[:, pl.ds((quarter * NB + block) * T, T)]
            for feature in range(2):
                columns_ref[first, pl.ds(feature * NB + block, 1), :] = piece[feature : feature + 1]
        whole = columns_ref[first]
        for z in range(4):
            for y in range(4):
                if z or y:
                    columns_ref[member(quarter, z, y)] = whole
    for copy in copies[1:]:
        copy.wait()

    def step(i, carry):
        for j in range(16):
            at = i * 16 + j
            place = index_ref[at]
            rows_ref[pl.ds(at, 1), :] = pool_ref[pl.ds(place, 1), :]
            column_ref[pl.ds(at, 1), :] = jnp.full((1, T), labels_ref[place].astype(F32), F32)
        return carry

    lax.fori_loop(0, OWN // 16, step, 0)
    flat = [column_ref[k * T : (k + 1) * T, :].T[0:1] for k in range(OWN // T)]
    rows_ref[OWN : OWN + 8, :] = jnp.concatenate(flat + [jnp.zeros((8 - OWN // T, T), F32)], axis=0)


def labels_kernel(quarter_ref, labels_ref, class_ref, out_ref):
    classes = class_ref.shape[0]
    own = labels_ref[pl.ds(pl.multiple_of(quarter_ref[0] * NB, NB), NB), :]
    kinds = class_ref[...] * (-SCALE)
    for block in range(NB):
        onehot = (lax.broadcasted_iota(jnp.int32, (classes, T), 0) == own[block : block + 1]).astype(F32)
        mapped = jnp.dot(kinds, onehot, precision=lax.Precision.HIGHEST, preferred_element_type=F32)
        mapped = jnp.concatenate([mapped, jnp.zeros((16 - classes, T), F32)], axis=0)
        hi, mid, low = split3(mapped)
        filled = jnp.concatenate([hi, mid, low, jnp.zeros((T - 48, T), BF16)], axis=0)
        out_ref[:, block * T : (block + 1) * T] = filled


def rows_block(load, piece_ref):
    for piece in range(T // 32):
        top, total = lse_list([load(block, piece * 32) for block in range(NB)])
        piece_ref[piece * 32 : (piece + 1) * 32, :] = top + jnp.log2(total)
    flat = piece_ref[...].T
    top = jnp.max(flat, axis=0, keepdims=True)
    return top + jnp.log2(jnp.sum(jnp.exp2(flat - top), axis=0, keepdims=True))


def group_costs(rows_ref, group, b, squares_v, cost_ref, part_ref, piece_ref):
    x = rows_ref[0:OWN, :]
    squares = jnp.sum(x * x, axis=1, keepdims=True) * (-SCALE / T)
    hi, mid, low = split3(x * (2.0 * SCALE / T))
    lane = lax.broadcasted_iota(jnp.int32, (OWN, T), 1)
    flat = [jnp.broadcast_to(rows_ref[OWN + k : OWN + k + 1, :], (T, T)).T for k in range(OWN // T)]
    label = jnp.concatenate(flat, axis=0).astype(jnp.int32)
    ext = jnp.where((lane % 16 == label) & (lane < 48), 1.0, 0.0).astype(BF16)
    a = jnp.concatenate([hi, hi, mid, hi, low, mid, ext], axis=1)
    start = pl.multiple_of(group * OWN, OWN)
    cost_ref[pl.ds(start, OWN), :] = jnp.dot(a, b, preferred_element_type=F32) + squares + squares_v
    for half in range(OWN // T):

        def load(block, row):
            return cost_ref[pl.ds(start + half * T + row, 32), block * T : (block + 1) * T]

        part_ref[pl.ds(group * 2 + half, 1), :] = rows_block(load, piece_ref.at[half])


def own_costs_kernel(rows_ref, val_ref, kinds_ref, cost_ref, part_ref, b_ref, squares_ref, piece_ref):
    for block in range(NB):
        lanes = slice(block * T, (block + 1) * T)
        y = val_ref[pl.ds(block, T, stride=NB), :]
        hi, mid, low = split3(y)
        for k, part in enumerate((hi, mid, hi, low, hi, mid)):
            b_ref[k * T : (k + 1) * T, lanes] = part
        squares_ref[:, lanes] = jnp.broadcast_to(jnp.sum(y * y, axis=0, keepdims=True) * (-SCALE / T), (8, T))
    b_ref[6 * T : 7 * T, :] = kinds_ref[...]
    group_costs(rows_ref, 0, b_ref[...], squares_ref[0:1, :], cost_ref, part_ref, piece_ref)


def other_costs_kernel(
    rows1_ref, rows2_ref, rows3_ref, b_ref, squares_ref, quarter_ref, own_ref, part_ref, cost_ref, out_ref, full_ref, piece_ref
):
    quarter = quarter_ref[0]
    full_ref[pl.ds(quarter * 2, 2), :] = part_ref[0:2, :]
    cost_ref[pl.ds(pl.multiple_of(quarter * OWN, OWN), OWN), :] = own_ref[...]
    for apart, rows_ref in enumerate((rows1_ref, rows2_ref, rows3_ref)):
        group = quarter ^ (apart + 1)
        group_costs(rows_ref, group, b_ref[...], squares_ref[0:1, :], cost_ref, full_ref, piece_ref.at[apart])
    send(full_ref, out_ref)


def rows_step_kernel(parts_ref, cost_ref, out_ref, piece_ref, part_ref):
    g = -15.0 - lse_lead(parts_ref)
    wide = [jnp.broadcast_to(g[block : block + 1], (32, T)) for block in range(NB)]
    for s in range(NB):

        def load(block, row):
            return cost_ref[s * T + row : s * T + row + 32, block * T : (block + 1) * T] + wide[block]

        part_ref[s : s + 1, :] = rows_block(load, piece_ref.at[s])
    send(part_ref, out_ref)


def columns_lse(f, cost_ref, wide_ref, part_ref):
    for s in range(NB):
        wide_ref[s * T : (s + 1) * T, :] = jnp.broadcast_to(f[s : s + 1], (T, T)).T
    for block in range(NB):
        lanes = slice(block * T, (block + 1) * T)
        tops, totals = [], []
        for start in range(0, SIDE, 64):
            rows = [slice(start + 8 * j, start + 8 * j + 8) for j in range(8)]
            top, total = lse_list([cost_ref[r, lanes] + wide_ref[r, :] for r in rows])
            tops.append(top)
            totals.append(total)
        best = jnp.max(tree(jnp.maximum, tops), axis=0, keepdims=True)
        total = tree(jnp.add, [total * jnp.exp2(top - best) for top, total in zip(tops, totals)])
        part_ref[block : block + 1, :] = best + jnp.log2(jnp.sum(total, axis=0, keepdims=True))


def columns_step_kernel(parts_ref, cost_ref, out_ref, wide_ref, part_ref):
    f = -14.0 - lse_lead(parts_ref)
    columns_lse(f, cost_ref, wide_ref, part_ref)
    send(part_ref, out_ref)


def last_columns_kernel(parts_ref, cost_ref, out_ref, f_ref, wide_ref, part_ref, row_ref):
    f = -14.0 - lse_lead(parts_ref)
    f_ref[...] = f
    columns_lse(f, cost_ref, wide_ref, part_ref)
    for block in range(NB):
        row_ref[:, block * T : (block + 1) * T] = part_ref[block : block + 1, :]
    row_ref[:, SIDE : SIDE + T] = jnp.sum(f, axis=0, keepdims=True)
    send(row_ref, out_ref)


def finish_kernel(parts_ref, f_ref, quarter_ref, value_ref, potential_ref):
    total = tree(jnp.add, [parts_ref[k, :, SIDE : SIDE + T] for k in range(parts_ref.shape[0])])
    mean = jnp.sum(total) * (0.25 / 16384.0)
    value_ref[...] = (f_ref[pl.ds(quarter_ref[0] * 2, 2), :] - mean) * BACK
    for quarter in range(4):
        parts = [parts_ref[member(quarter, z, y), :, 0:SIDE] for z in range(4) for y in range(4)]
        top, whole = lse_list(parts)
        potential_ref[quarter] = (-15.0 - (top + jnp.log2(whole))) * BACK


SPEC = pl.BlockSpec(memory_space=pltpu.VMEM)
SCALARS = pl.BlockSpec(memory_space=pltpu.SMEM)
FAR = pl.BlockSpec(memory_space=pltpu.HBM)


def vmem(shape, dtype=F32):
    return pltpu.VMEM(shape, dtype)


def shape(dims, dtype=F32):
    return jax.ShapeDtypeStruct(dims, dtype)


def call(kernel, out, ins, scratch=()):
    return pl.pallas_call(
        kernel,
        out_shape=out,
        in_specs=ins,
        out_specs=[SPEC] * len(out),
        scratch_shapes=list(scratch),
        compiler_params=PARAMS,
    )


def local(pool, window_index, pool_labels, val_embed, val_labels, class_cost):
    quarter = lax.axis_index(QUAD).astype(jnp.int32).reshape(1)
    columns, rows = call(
        prepare_kernel,
        [shape((64, 16, T)), shape((OWN + 8, T))],
        [FAR] * 4,
        [
            pltpu.SMEM(window_index.shape, jnp.int32),
            pltpu.SMEM(pool_labels.shape, jnp.int32),
            vmem(pool.shape),
            vmem((2, 4096)),
            vmem((OWN, T)),
            pltpu.SemaphoreType.DMA((4,)),
        ],
    )(*[pltpu.with_memory_space_constraint(x, pltpu.HBM) for x in (window_index, pool_labels, pool, val_embed.T)])
    columns = lax.all_to_all(columns, ROW, 0, 0)
    others = [lax.ppermute(rows, QUAD, [(i, i ^ apart) for i in range(4)]) for apart in (1, 2, 3)]
    rows, val_labels, class_cost = lax.optimization_barrier((rows, val_labels, class_cost))
    (kinds,) = call(labels_kernel, [shape((T, SIDE), BF16)], [SCALARS, SPEC, SPEC])(
        quarter, val_labels.reshape(32, T), class_cost
    )
    part, piece, wide = vmem((NB, T)), vmem((NB, T, T)), vmem((SIDE, T))
    own, part_own, b, squares = call(
        own_costs_kernel,
        [shape((OWN, SIDE)), shape((NB, T)), shape((7 * T, SIDE), BF16), shape((8, SIDE))],
        [SPEC] * 3,
        [vmem((2, T, T))],
    )(rows, columns.reshape(SIDE, T), kinds)
    cost, parts = call(
        other_costs_kernel,
        [shape((SIDE, SIDE)), shape((32, NB, T))],
        [SPEC] * 5 + [SCALARS] + [SPEC] * 2,
        [part, vmem((3, 2, T, T))],
    )(*others, b, squares, quarter, own, part_own)
    parts = lax.all_to_all(parts, ALONG, 0, 0)
    (parts,) = call(columns_step_kernel, [shape((16, NB, T))], [SPEC] * 2, [wide, part])(parts, cost)
    parts = lax.all_to_all(parts, ACROSS, 0, 0)
    (parts,) = call(rows_step_kernel, [shape((32, NB, T))], [SPEC] * 2, [piece, part])(parts, cost)
    parts = lax.all_to_all(parts, ALONG, 0, 0)
    parts, f = call(
        last_columns_kernel, [shape((64, 1, SIDE + T)), shape((NB, T))], [SPEC] * 2, [wide, part, vmem((1, SIDE + T))]
    )(parts, cost)
    parts = lax.all_to_all(parts, ROW, 0, 0)
    value, potential = call(finish_kernel, [shape((2, T)), shape((4, 1, SIDE))], [SPEC, SPEC, SCALARS])(parts, f, quarter)
    return value.reshape(256), potential.reshape(4096)


def solution(mesh):
    fine = Mesh(mesh.devices.reshape(2, 2, 2, 2, 2, 2, 4, 2), ROW + COL)
    placed = (P(ROW, None), P(ROW), P(ROW), P(COL, ROW), P(COL), P())
    return jax.shard_map(local, mesh=fine, in_specs=placed, out_specs=(P(ROW), P(COL)), check_vma=False)
```

```python
import math

import jax
import jax.numpy as jnp
from jax import lax
from jax.experimental import pallas as pl
from jax.experimental.pallas import tpu as pltpu
from jax.sharding import Mesh
from jax.sharding import PartitionSpec as P

EPSILON = 0.02
SCALE = 1.0 / (EPSILON * math.log(2.0))
BACK = EPSILON * math.log(2.0)

ROW = ("z2", "z1", "z0", "y2", "y1", "y0")
COL = ("x", "core")
QUAD = ("z0", "y0")
ACROSS = ("z2", "z1", "y2", "y1")
ALONG = QUAD + COL

FIRST = (6, 4)
LATER = (4, 4)


def turned(z_size, y_size, z_first, y_first):
    return [[(z + z_first) % z_size * y_size + (y + y_first) % y_size for z in range(z_size) for y in range(y_size)]]


FIRST_ROW_ORDER = turned(8, 8, *FIRST)
ROW_ORDER = turned(8, 8, *LATER)
ACROSS_ORDER = turned(4, 4, LATER[0] // 2, LATER[1] // 2)
ALONG_ORDER = [[(quarter ^ 3) * 8 + (x + 2) % 4 * 2 + core for quarter in range(4) for x in range(4) for core in range(2)]]

T = 128
NB = 8
SIDE = NB * T
OWN = 256
PARAMS = pltpu.CompilerParams(vmem_limit_bytes=20 * 1024 * 1024)
F32 = jnp.float32
BF16 = jnp.bfloat16


def split3(x):
    hi = x.astype(BF16)
    rest = x - hi.astype(F32)
    mid = rest.astype(BF16)
    low = (rest - mid.astype(F32)).astype(BF16)
    return hi, mid, low


def member(quarter, z, y):
    return ((z * 2 + quarter // 2) * 4 + y) * 2 + quarter % 2


def in_order(y):
    places = [(z - FIRST[0]) % 8 * 2 + (half - FIRST[1] // 4) % 2 for z in range(8) for half in range(2)]
    return jnp.concatenate([y[8 * place : 8 * place + 8] for place in places], axis=0)


def tree(op, xs):
    xs = list(xs)
    while len(xs) > 1:
        xs = [op(*xs[i : i + 2]) if i + 1 < len(xs) else xs[i] for i in range(0, len(xs), 2)]
    return xs[0]


def lse_list(zs):
    top = tree(jnp.maximum, zs)
    return top, tree(jnp.add, [jnp.exp2(z - top) for z in zs])


def lse_lead(parts_ref):
    top, total = lse_list([parts_ref[k] for k in range(parts_ref.shape[0])])
    return top + jnp.log2(total)


def send(part_ref, out_ref):
    part = part_ref[...]
    for k in range(out_ref.shape[0]):
        out_ref[k] = part


def columns_kernel(val_hbm, columns_ref, val_ref, sem):
    copy = pltpu.make_async_copy(val_hbm, val_ref, sem)
    copy.start()
    copy.wait()
    for quarter in range(4):
        first = member(quarter, 0, 0)
        for block in range(NB):
            piece = val_ref[:, pl.ds((quarter * NB + block) * T, T)]
            for feature in range(2):
                columns_ref[first, pl.ds(feature * NB + block, 1), :] = piece[feature : feature + 1]
        whole = columns_ref[first]
        for z in range(4):
            for y in range(4):
                if z or y:
                    columns_ref[member(quarter, z, y)] = whole


def rows_kernel(index_hbm, labels_hbm, pool_hbm, rows_ref, index_ref, labels_ref, pool_ref, column_ref, sems):
    moves = [(index_hbm, index_ref), (labels_hbm, labels_ref), (pool_hbm, pool_ref)]
    copies = [pltpu.make_async_copy(a, b, sems.at[k]) for k, (a, b) in enumerate(moves)]
    for copy in copies:
        copy.start()
    for copy in copies:
        copy.wait()

    def step(i, carry):
        for j in range(16):
            at = i * 16 + j
            place = index_ref[at]
            rows_ref[pl.ds(at, 1), :] = pool_ref[pl.ds(place, 1), :]
            column_ref[pl.ds(at, 1), :] = jnp.full((1, T), labels_ref[place].astype(F32), F32)
        return carry

    lax.fori_loop(0, OWN // 16, step, 0)
    flat = [column_ref[k * T : (k + 1) * T, :].T[0:1] for k in range(OWN // T)]
    rows_ref[OWN : OWN + 8, :] = jnp.concatenate(flat + [jnp.zeros((8 - OWN // T, T), F32)], axis=0)


def labels_kernel(quarter_ref, labels_ref, class_ref, out_ref):
    classes = class_ref.shape[0]
    own = labels_ref[pl.ds(pl.multiple_of(quarter_ref[0] * NB, NB), NB), :]
    kinds = class_ref[...] * (-SCALE)
    for block in range(NB):
        onehot = (lax.broadcasted_iota(jnp.int32, (classes, T), 0) == own[block : block + 1]).astype(F32)
        mapped = jnp.dot(kinds, onehot, precision=lax.Precision.HIGHEST, preferred_element_type=F32)
        mapped = jnp.concatenate([mapped, jnp.zeros((16 - classes, T), F32)], axis=0)
        hi, mid, low = split3(mapped)
        filled = jnp.concatenate([hi, mid, low, jnp.zeros((T - 48, T), BF16)], axis=0)
        out_ref[:, block * T : (block + 1) * T] = filled


def rows_block(load, piece_ref):
    for piece in range(T // 32):
        top, total = lse_list([load(block, piece * 32) for block in range(NB)])
        piece_ref[piece * 32 : (piece + 1) * 32, :] = top + jnp.log2(total)
    flat = piece_ref[...].T
    top = jnp.max(flat, axis=0, keepdims=True)
    return top + jnp.log2(jnp.sum(jnp.exp2(flat - top), axis=0, keepdims=True))


def group_costs(rows_ref, group, b, squares_v, cost_ref, part_ref, piece_ref):
    x = rows_ref[0:OWN, :]
    squares = jnp.sum(x * x, axis=1, keepdims=True) * (-SCALE / T)
    hi, mid, low = split3(x * (2.0 * SCALE / T))
    lane = lax.broadcasted_iota(jnp.int32, (OWN, T), 1)
    flat = [jnp.broadcast_to(rows_ref[OWN + k : OWN + k + 1, :], (T, T)).T for k in range(OWN // T)]
    label = jnp.concatenate(flat, axis=0).astype(jnp.int32)
    ext = jnp.where((lane % 16 == label) & (lane < 48), 1.0, 0.0).astype(BF16)
    a = jnp.concatenate([hi, hi, mid, hi, low, mid, ext], axis=1)
    start = pl.multiple_of(group * OWN, OWN)
    cost_ref[pl.ds(start, OWN), :] = jnp.dot(a, b, preferred_element_type=F32) + squares + squares_v
    for half in range(OWN // T):

        def load(block, row):
            return cost_ref[pl.ds(start + half * T + row, 32), block * T : (block + 1) * T]

        part_ref[pl.ds(group * 2 + half, 1), :] = rows_block(load, piece_ref.at[half])


def own_costs_kernel(rows_ref, val_ref, kinds_ref, cost_ref, part_ref, b_ref, squares_ref, piece_ref):
    for block in range(NB):
        lanes = slice(block * T, (block + 1) * T)
        y = in_order(val_ref[pl.ds(block, T, stride=NB), :])
        hi, mid, low = split3(y)
        for k, part in enumerate((hi, mid, hi, low, hi, mid)):
            b_ref[k * T : (k + 1) * T, lanes] = part
        squares_ref[:, lanes] = jnp.broadcast_to(jnp.sum(y * y, axis=0, keepdims=True) * (-SCALE / T), (8, T))
    b_ref[6 * T : 7 * T, :] = kinds_ref[...]
    group_costs(rows_ref, 0, b_ref[...], squares_ref[0:1, :], cost_ref, part_ref, piece_ref)


def other_costs_kernel(
    rows1_ref, rows2_ref, rows3_ref, b_ref, squares_ref, quarter_ref, own_ref, part_ref, cost_ref, out_ref, full_ref, piece_ref
):
    quarter = quarter_ref[0]
    full_ref[pl.ds(quarter * 2, 2), :] = part_ref[0:2, :]
    cost_ref[pl.ds(pl.multiple_of(quarter * OWN, OWN), OWN), :] = own_ref[...]
    for apart, rows_ref in enumerate((rows1_ref, rows2_ref, rows3_ref)):
        group = quarter ^ (apart + 1)
        group_costs(rows_ref, group, b_ref[...], squares_ref[0:1, :], cost_ref, full_ref, piece_ref.at[apart])
    send(full_ref, out_ref)


def rows_step_kernel(parts_ref, cost_ref, out_ref, piece_ref, part_ref):
    g = -15.0 - lse_lead(parts_ref)
    wide = [jnp.broadcast_to(g[block : block + 1], (32, T)) for block in range(NB)]
    for s in range(NB):

        def load(block, row):
            return cost_ref[s * T + row : s * T + row + 32, block * T : (block + 1) * T] + wide[block]

        part_ref[s : s + 1, :] = rows_block(load, piece_ref.at[s])
    send(part_ref, out_ref)


def columns_lse(f, cost_ref, wide_ref, part_ref):
    for s in range(NB):
        wide_ref[s * T : (s + 1) * T, :] = jnp.broadcast_to(f[s : s + 1], (T, T)).T
    for block in range(NB):
        lanes = slice(block * T, (block + 1) * T)
        tops, totals = [], []
        for start in range(0, SIDE, 64):
            rows = [slice(start + 8 * j, start + 8 * j + 8) for j in range(8)]
            top, total = lse_list([cost_ref[r, lanes] + wide_ref[r, :] for r in rows])
            tops.append(top)
            totals.append(total)
        best = jnp.max(tree(jnp.maximum, tops), axis=0, keepdims=True)
        total = tree(jnp.add, [total * jnp.exp2(top - best) for top, total in zip(tops, totals)])
        part_ref[block : block + 1, :] = best + jnp.log2(jnp.sum(total, axis=0, keepdims=True))


def columns_step_kernel(parts_ref, cost_ref, out_ref, wide_ref, part_ref):
    f = -14.0 - lse_lead(parts_ref)
    columns_lse(f, cost_ref, wide_ref, part_ref)
    send(part_ref, out_ref)


def last_columns_kernel(parts_ref, cost_ref, out_ref, f_ref, wide_ref, part_ref, row_ref):
    f = -14.0 - lse_lead(parts_ref)
    f_ref[...] = f
    columns_lse(f, cost_ref, wide_ref, part_ref)
    for block in range(NB):
        row_ref[:, block * T : (block + 1) * T] = part_ref[block : block + 1, :]
    row_ref[:, SIDE : SIDE + T] = jnp.sum(f, axis=0, keepdims=True)
    send(row_ref, out_ref)


def finish_kernel(parts_ref, f_ref, quarter_ref, value_ref, potential_ref):
    total = tree(jnp.add, [parts_ref[k, :, SIDE : SIDE + T] for k in range(parts_ref.shape[0])])
    mean = jnp.sum(total) * (0.25 / 16384.0)
    value_ref[...] = (f_ref[pl.ds(quarter_ref[0] * 2, 2), :] - mean) * BACK
    for quarter in range(4):
        parts = [parts_ref[member(quarter, z, y), :, 0:SIDE] for z in range(4) for y in range(4)]
        top, whole = lse_list(parts)
        potential_ref[quarter] = (-15.0 - (top + jnp.log2(whole))) * BACK


SPEC = pl.BlockSpec(memory_space=pltpu.VMEM)
SCALARS = pl.BlockSpec(memory_space=pltpu.SMEM)
FAR = pl.BlockSpec(memory_space=pltpu.HBM)


def vmem(shape, dtype=F32):
    return pltpu.VMEM(shape, dtype)


def far(x):
    return pltpu.with_memory_space_constraint(x, pltpu.HBM)


def shape(dims, dtype=F32):
    return jax.ShapeDtypeStruct(dims, dtype)


def call(kernel, out, ins, scratch=()):
    return pl.pallas_call(
        kernel,
        out_shape=out,
        in_specs=ins,
        out_specs=[SPEC] * len(out),
        scratch_shapes=list(scratch),
        compiler_params=PARAMS,
    )


def local(pool, window_index, pool_labels, val_embed, val_labels, class_cost):
    quarter = lax.axis_index(QUAD).astype(jnp.int32).reshape(1)
    (columns,) = call(
        columns_kernel, [shape((64, 16, T))], [FAR], [vmem((2, 4096)), pltpu.SemaphoreType.DMA(())]
    )(far(val_embed.T))
    columns, window_index = lax.optimization_barrier((columns, window_index))
    (rows,) = call(
        rows_kernel,
        [shape((OWN + 8, T))],
        [FAR] * 3,
        [
            pltpu.SMEM(window_index.shape, jnp.int32),
            pltpu.SMEM(pool_labels.shape, jnp.int32),
            vmem(pool.shape),
            vmem((OWN, T)),
            pltpu.SemaphoreType.DMA((3,)),
        ],
    )(far(window_index), far(pool_labels), far(pool))
    columns = lax.all_to_all(columns, ROW, 0, 0, axis_index_groups=FIRST_ROW_ORDER)
    others = [lax.ppermute(rows, QUAD, [(i, i ^ apart) for i in range(4)]) for apart in (1, 2, 3)]
    rows, val_labels, class_cost = lax.optimization_barrier((rows, val_labels, class_cost))
    (kinds,) = call(labels_kernel, [shape((T, SIDE), BF16)], [SCALARS, SPEC, SPEC])(
        quarter, val_labels.reshape(32, T), class_cost
    )
    part, piece, wide = vmem((NB, T)), vmem((NB, T, T)), vmem((SIDE, T))
    own, part_own, b, squares = call(
        own_costs_kernel,
        [shape((OWN, SIDE)), shape((NB, T)), shape((7 * T, SIDE), BF16), shape((8, SIDE))],
        [SPEC] * 3,
        [vmem((2, T, T))],
    )(rows, columns.reshape(SIDE, T), kinds)
    cost, parts = call(
        other_costs_kernel,
        [shape((SIDE, SIDE)), shape((32, NB, T))],
        [SPEC] * 5 + [SCALARS] + [SPEC] * 2,
        [part, vmem((3, 2, T, T))],
    )(*others, b, squares, quarter, own, part_own)
    parts = lax.all_to_all(parts, ALONG, 0, 0, axis_index_groups=ALONG_ORDER)
    (parts,) = call(columns_step_kernel, [shape((16, NB, T))], [SPEC] * 2, [wide, part])(parts, cost)
    parts = lax.all_to_all(parts, ACROSS, 0, 0, axis_index_groups=ACROSS_ORDER)
    (parts,) = call(rows_step_kernel, [shape((32, NB, T))], [SPEC] * 2, [piece, part])(parts, cost)
    parts = lax.all_to_all(parts, ALONG, 0, 0, axis_index_groups=ALONG_ORDER)
    parts, f = call(
        last_columns_kernel, [shape((64, 1, SIDE + T)), shape((NB, T))], [SPEC] * 2, [wide, part, vmem((1, SIDE + T))]
    )(parts, cost)
    parts = lax.all_to_all(parts, ROW, 0, 0, axis_index_groups=ROW_ORDER)
    value, potential = call(finish_kernel, [shape((2, T)), shape((4, 1, SIDE))], [SPEC, SPEC, SCALARS])(parts, f, quarter)
    return value.reshape(256), potential.reshape(4096)


def solution(mesh):
    fine = Mesh(mesh.devices.reshape(2, 2, 2, 2, 2, 2, 4, 2), ROW + COL)
    placed = (P(ROW, None), P(ROW), P(ROW), P(COL, ROW), P(COL), P())
    return jax.shard_map(local, mesh=fine, in_specs=placed, out_specs=(P(ROW), P(COL)), check_vma=False)
```

```python
import math

import jax
import jax.numpy as jnp
from jax import lax
from jax.experimental import pallas as pl
from jax.experimental.pallas import tpu as pltpu
from jax.sharding import Mesh
from jax.sharding import PartitionSpec as P

EPSILON = 0.02
SCALE = 1.0 / (EPSILON * math.log(2.0))
BACK = EPSILON * math.log(2.0)

ROW = ("z2", "z1", "z0", "y2", "y1", "y0")
COL = ("x", "core")
QUAD = ("z0", "y0")
ACROSS = ("z2", "z1", "y2", "y1")
ALONG = QUAD + COL

FIRST = (4, 4)


def turned(z_size, y_size, z_first, y_first):
    return [[(z + z_first) % z_size * y_size + (y + y_first) % y_size for z in range(z_size) for y in range(y_size)]]


ROW_ORDER = turned(8, 8, *FIRST)
ACROSS_ORDER = turned(4, 4, FIRST[0] // 2, FIRST[1] // 2)
ALONG_ORDER = [[(quarter ^ 3) * 8 + (x + 2) % 4 * 2 + (1 - core) for quarter in range(4) for x in range(4) for core in range(2)]]

T = 128
NB = 8
SIDE = NB * T
OWN = 256
PARAMS = pltpu.CompilerParams(vmem_limit_bytes=20 * 1024 * 1024)
F32 = jnp.float32
BF16 = jnp.bfloat16


def split3(x):
    hi = x.astype(BF16)
    rest = x - hi.astype(F32)
    mid = rest.astype(BF16)
    low = (rest - mid.astype(F32)).astype(BF16)
    return hi, mid, low


def member(quarter, z, y):
    return ((z * 2 + quarter // 2) * 4 + y) * 2 + quarter % 2


def in_order(y):
    places = [(z - FIRST[0]) % 8 * 2 + (half - FIRST[1] // 4) % 2 for z in range(8) for half in range(2)]
    return jnp.concatenate([y[8 * place : 8 * place + 8] for place in places], axis=0)


def tree(op, xs):
    xs = list(xs)
    while len(xs) > 1:
        xs = [op(*xs[i : i + 2]) if i + 1 < len(xs) else xs[i] for i in range(0, len(xs), 2)]
    return xs[0]


def lse_list(zs):
    top = tree(jnp.maximum, zs)
    return top, tree(jnp.add, [jnp.exp2(z - top) for z in zs])


def lse_lead(parts_ref):
    top, total = lse_list([parts_ref[k] for k in range(parts_ref.shape[0])])
    return top + jnp.log2(total)


def send(part_ref, out_ref):
    part = part_ref[...]
    for k in range(out_ref.shape[0]):
        out_ref[k] = part


def columns_kernel(val_hbm, columns_ref, val_ref, sem):
    copy = pltpu.make_async_copy(val_hbm, val_ref, sem)
    copy.start()
    copy.wait()
    for quarter in range(4):
        first = member(quarter, 0, 0)
        for block in range(NB):
            piece = val_ref[:, pl.ds((quarter * NB + block) * T, T)]
            for feature in range(2):
                columns_ref[first, pl.ds(feature * NB + block, 1), :] = piece[feature : feature + 1]
        whole = columns_ref[first]
        for z in range(4):
            for y in range(4):
                if z or y:
                    columns_ref[member(quarter, z, y)] = whole


def rows_kernel(index_hbm, labels_hbm, pool_hbm, rows_ref, index_ref, labels_ref, pool_ref, column_ref, sems):
    moves = [(index_hbm, index_ref), (labels_hbm, labels_ref), (pool_hbm, pool_ref)]
    copies = [pltpu.make_async_copy(a, b, sems.at[k]) for k, (a, b) in enumerate(moves)]
    for copy in copies:
        copy.start()
    for copy in copies:
        copy.wait()

    def step(i, carry):
        for j in range(16):
            at = i * 16 + j
            place = index_ref[at]
            rows_ref[pl.ds(at, 1), :] = pool_ref[pl.ds(place, 1), :]
            column_ref[pl.ds(at, 1), :] = jnp.full((1, T), labels_ref[place].astype(F32), F32)
        return carry

    lax.fori_loop(0, OWN // 16, step, 0)
    flat = [column_ref[k * T : (k + 1) * T, :].T[0:1] for k in range(OWN // T)]
    rows_ref[OWN : OWN + 8, :] = jnp.concatenate(flat + [jnp.zeros((8 - OWN // T, T), F32)], axis=0)


def labels_kernel(quarter_ref, labels_ref, class_ref, out_ref):
    classes = class_ref.shape[0]
    own = labels_ref[pl.ds(pl.multiple_of(quarter_ref[0] * NB, NB), NB), :]
    kinds = class_ref[...] * (-SCALE)
    for block in range(NB):
        onehot = (lax.broadcasted_iota(jnp.int32, (classes, T), 0) == own[block : block + 1]).astype(F32)
        mapped = jnp.dot(kinds, onehot, precision=lax.Precision.HIGHEST, preferred_element_type=F32)
        mapped = jnp.concatenate([mapped, jnp.zeros((16 - classes, T), F32)], axis=0)
        hi, mid, low = split3(mapped)
        filled = jnp.concatenate([hi, mid, low, jnp.zeros((T - 48, T), BF16)], axis=0)
        out_ref[:, block * T : (block + 1) * T] = filled


def rows_block(load, piece_ref):
    for piece in range(T // 32):
        top, total = lse_list([load(block, piece * 32) for block in range(NB)])
        piece_ref[piece * 32 : (piece + 1) * 32, :] = top + jnp.log2(total)
    flat = piece_ref[...].T
    top = jnp.max(flat, axis=0, keepdims=True)
    return top + jnp.log2(jnp.sum(jnp.exp2(flat - top), axis=0, keepdims=True))


def group_costs(rows_ref, group, b, squares_v, cost_ref, part_ref, piece_ref):
    x = rows_ref[0:OWN, :]
    squares = jnp.sum(x * x, axis=1, keepdims=True) * (-SCALE / T)
    hi, mid, low = split3(x * (2.0 * SCALE / T))
    lane = lax.broadcasted_iota(jnp.int32, (OWN, T), 1)
    flat = [jnp.broadcast_to(rows_ref[OWN + k : OWN + k + 1, :], (T, T)).T for k in range(OWN // T)]
    label = jnp.concatenate(flat, axis=0).astype(jnp.int32)
    ext = jnp.where((lane % 16 == label) & (lane < 48), 1.0, 0.0).astype(BF16)
    a = jnp.concatenate([hi, hi, mid, hi, low, mid, ext], axis=1)
    start = pl.multiple_of(group * OWN, OWN)
    cost_ref[pl.ds(start, OWN), :] = jnp.dot(a, b, preferred_element_type=F32) + squares + squares_v
    for half in range(OWN // T):

        def load(block, row):
            return cost_ref[pl.ds(start + half * T + row, 32), block * T : (block + 1) * T]

        part_ref[pl.ds(group * 2 + half, 1), :] = rows_block(load, piece_ref.at[half])


def own_costs_kernel(rows_ref, val_ref, kinds_ref, cost_ref, part_ref, b_ref, squares_ref, piece_ref):
    for block in range(NB):
        lanes = slice(block * T, (block + 1) * T)
        y = in_order(val_ref[pl.ds(block, T, stride=NB), :])
        hi, mid, low = split3(y)
        for k, part in enumerate((hi, mid, hi, low, hi, mid)):
            b_ref[k * T : (k + 1) * T, lanes] = part
        squares_ref[:, lanes] = jnp.broadcast_to(jnp.sum(y * y, axis=0, keepdims=True) * (-SCALE / T), (8, T))
    b_ref[6 * T : 7 * T, :] = kinds_ref[...]
    group_costs(rows_ref, 0, b_ref[...], squares_ref[0:1, :], cost_ref, part_ref, piece_ref)


def other_costs_kernel(
    rows1_ref, rows2_ref, rows3_ref, b_ref, squares_ref, quarter_ref, own_ref, part_ref, cost_ref, out_ref, full_ref, piece_ref
):
    quarter = quarter_ref[0]
    full_ref[pl.ds(quarter * 2, 2), :] = part_ref[0:2, :]
    cost_ref[pl.ds(pl.multiple_of(quarter * OWN, OWN), OWN), :] = own_ref[...]
    for apart, rows_ref in enumerate((rows1_ref, rows2_ref, rows3_ref)):
        group = quarter ^ (apart + 1)
        group_costs(rows_ref, group, b_ref[...], squares_ref[0:1, :], cost_ref, full_ref, piece_ref.at[apart])
    send(full_ref, out_ref)


def rows_step_kernel(parts_ref, cost_ref, out_ref, piece_ref, part_ref):
    g = -15.0 - lse_lead(parts_ref)
    wide = [jnp.broadcast_to(g[block : block + 1], (32, T)) for block in range(NB)]
    for s in range(NB):

        def load(block, row):
            return cost_ref[s * T + row : s * T + row + 32, block * T : (block + 1) * T] + wide[block]

        part_ref[s : s + 1, :] = rows_block(load, piece_ref.at[s])
    send(part_ref, out_ref)


def columns_lse(f, cost_ref, wide_ref, part_ref):
    for s in range(NB):
        wide_ref[s * T : (s + 1) * T, :] = jnp.broadcast_to(f[s : s + 1], (T, T)).T
    for block in range(NB):
        lanes = slice(block * T, (block + 1) * T)
        tops, totals = [], []
        for start in range(0, SIDE, 64):
            rows = [slice(start + 8 * j, start + 8 * j + 8) for j in range(8)]
            top, total = lse_list([cost_ref[r, lanes] + wide_ref[r, :] for r in rows])
            tops.append(top)
            totals.append(total)
        best = jnp.max(tree(jnp.maximum, tops), axis=0, keepdims=True)
        total = tree(jnp.add, [total * jnp.exp2(top - best) for top, total in zip(tops, totals)])
        part_ref[block : block + 1, :] = best + jnp.log2(jnp.sum(total, axis=0, keepdims=True))


def columns_step_kernel(parts_ref, cost_ref, out_ref, wide_ref, part_ref):
    f = -14.0 - lse_lead(parts_ref)
    columns_lse(f, cost_ref, wide_ref, part_ref)
    send(part_ref, out_ref)


def last_columns_kernel(parts_ref, cost_ref, out_ref, f_ref, wide_ref, part_ref, row_ref):
    f = -14.0 - lse_lead(parts_ref)
    f_ref[...] = f
    columns_lse(f, cost_ref, wide_ref, part_ref)
    for block in range(NB):
        row_ref[:, block * T : (block + 1) * T] = part_ref[block : block + 1, :]
    row_ref[:, SIDE : SIDE + T] = jnp.sum(f, axis=0, keepdims=True)
    send(row_ref, out_ref)


def finish_kernel(parts_ref, f_ref, quarter_ref, value_ref, potential_ref):
    total = tree(jnp.add, [parts_ref[k, :, SIDE : SIDE + T] for k in range(parts_ref.shape[0])])
    mean = jnp.sum(total) * (0.25 / 16384.0)
    value_ref[...] = (f_ref[pl.ds(quarter_ref[0] * 2, 2), :] - mean) * BACK
    for quarter in range(4):
        parts = [parts_ref[member(quarter, z, y), :, 0:SIDE] for z in range(4) for y in range(4)]
        top, whole = lse_list(parts)
        potential_ref[quarter] = (-15.0 - (top + jnp.log2(whole))) * BACK


SPEC = pl.BlockSpec(memory_space=pltpu.VMEM)
SCALARS = pl.BlockSpec(memory_space=pltpu.SMEM)
FAR = pl.BlockSpec(memory_space=pltpu.HBM)


def vmem(shape, dtype=F32):
    return pltpu.VMEM(shape, dtype)


def far(x):
    return pltpu.with_memory_space_constraint(x, pltpu.HBM)


def shape(dims, dtype=F32):
    return jax.ShapeDtypeStruct(dims, dtype)


def call(kernel, out, ins, scratch=()):
    return pl.pallas_call(
        kernel,
        out_shape=out,
        in_specs=ins,
        out_specs=[SPEC] * len(out),
        scratch_shapes=list(scratch),
        compiler_params=PARAMS,
    )


def local(pool, window_index, pool_labels, val_embed, val_labels, class_cost):
    quarter = lax.axis_index(QUAD).astype(jnp.int32).reshape(1)
    (columns,) = call(
        columns_kernel, [shape((64, 16, T))], [FAR], [vmem((2, 4096)), pltpu.SemaphoreType.DMA(())]
    )(far(val_embed.T))
    columns, window_index = lax.optimization_barrier((columns, window_index))
    (rows,) = call(
        rows_kernel,
        [shape((OWN + 8, T))],
        [FAR] * 3,
        [
            pltpu.SMEM(window_index.shape, jnp.int32),
            pltpu.SMEM(pool_labels.shape, jnp.int32),
            vmem(pool.shape),
            vmem((OWN, T)),
            pltpu.SemaphoreType.DMA((3,)),
        ],
    )(far(window_index), far(pool_labels), far(pool))
    columns = lax.all_to_all(columns, ROW, 0, 0, axis_index_groups=ROW_ORDER)
    others = [lax.ppermute(rows, QUAD, [(i, i ^ apart) for i in range(4)]) for apart in (1, 2, 3)]
    rows, val_labels, class_cost = lax.optimization_barrier((rows, val_labels, class_cost))
    (kinds,) = call(labels_kernel, [shape((T, SIDE), BF16)], [SCALARS, SPEC, SPEC])(
        quarter, val_labels.reshape(32, T), class_cost
    )
    part, piece, wide = vmem((NB, T)), vmem((NB, T, T)), vmem((SIDE, T))
    own, part_own, b, squares = call(
        own_costs_kernel,
        [shape((OWN, SIDE)), shape((NB, T)), shape((7 * T, SIDE), BF16), shape((8, SIDE))],
        [SPEC] * 3,
        [vmem((2, T, T))],
    )(rows, columns.reshape(SIDE, T), kinds)
    cost, parts = call(
        other_costs_kernel,
        [shape((SIDE, SIDE)), shape((32, NB, T))],
        [SPEC] * 5 + [SCALARS] + [SPEC] * 2,
        [part, vmem((3, 2, T, T))],
    )(*others, b, squares, quarter, own, part_own)
    parts = lax.all_to_all(parts, ALONG, 0, 0, axis_index_groups=ALONG_ORDER)
    (parts,) = call(columns_step_kernel, [shape((16, NB, T))], [SPEC] * 2, [wide, part])(parts, cost)
    parts = lax.all_to_all(parts, ACROSS, 0, 0, axis_index_groups=ACROSS_ORDER)
    (parts,) = call(rows_step_kernel, [shape((32, NB, T))], [SPEC] * 2, [piece, part])(parts, cost)
    parts = lax.all_to_all(parts, ALONG, 0, 0, axis_index_groups=ALONG_ORDER)
    parts, f = call(
        last_columns_kernel, [shape((64, 1, SIDE + T)), shape((NB, T))], [SPEC] * 2, [wide, part, vmem((1, SIDE + T))]
    )(parts, cost)
    parts = lax.all_to_all(parts, ROW, 0, 0, axis_index_groups=ROW_ORDER)
    value, potential = call(finish_kernel, [shape((2, T)), shape((4, 1, SIDE))], [SPEC, SPEC, SCALARS])(parts, f, quarter)
    return value.reshape(256), potential.reshape(4096)


def solution(mesh):
    fine = Mesh(mesh.devices.reshape(2, 2, 2, 2, 2, 2, 4, 2), ROW + COL)
    placed = (P(ROW, None), P(ROW), P(ROW), P(COL, ROW), P(COL), P())
    return jax.shard_map(local, mesh=fine, in_specs=placed, out_specs=(P(ROW), P(COL)), check_vma=False)
```

```python
import math

import jax
import jax.numpy as jnp
from jax import lax
from jax.experimental import pallas as pl
from jax.experimental.pallas import tpu as pltpu
from jax.sharding import Mesh
from jax.sharding import PartitionSpec as P

EPSILON = 0.02
SCALE = 1.0 / (EPSILON * math.log(2.0))
BACK = EPSILON * math.log(2.0)

ROW = ("z2", "z1", "z0", "y2", "y1", "y0")
COL = ("x", "core")
QUAD = ("z0", "y0")
ACROSS = ("z2", "z1", "y2", "y1")
ALONG = QUAD + COL

FIRST = (4, 4)


def turned(z_size, y_size, z_first, y_first):
    return [[(z + z_first) % z_size * y_size + (y + y_first) % y_size for z in range(z_size) for y in range(y_size)]]


ROW_ORDER = turned(8, 8, *FIRST)
ACROSS_ORDER = turned(4, 4, FIRST[0] // 2, FIRST[1] // 2)
ALONG_ORDER = [[(quarter ^ 3) * 8 + (x + 2) % 4 * 2 + (1 - core) for quarter in range(4) for x in range(4) for core in range(2)]]

T = 128
NB = 8
SIDE = NB * T
OWN = 256
PARAMS = pltpu.CompilerParams(vmem_limit_bytes=20 * 1024 * 1024)
F32 = jnp.float32
BF16 = jnp.bfloat16


def split3(x):
    hi = x.astype(BF16)
    rest = x - hi.astype(F32)
    mid = rest.astype(BF16)
    low = (rest - mid.astype(F32)).astype(BF16)
    return hi, mid, low


def member(quarter, z, y):
    return ((z * 2 + quarter // 2) * 4 + y) * 2 + quarter % 2


def in_order(y):
    places = [(z - FIRST[0]) % 8 * 2 + (half - FIRST[1] // 4) % 2 for z in range(8) for half in range(2)]
    return jnp.concatenate([y[8 * place : 8 * place + 8] for place in places], axis=0)


def tree(op, xs):
    xs = list(xs)
    while len(xs) > 1:
        xs = [op(*xs[i : i + 2]) if i + 1 < len(xs) else xs[i] for i in range(0, len(xs), 2)]
    return xs[0]


def lse_list(zs):
    top = tree(jnp.maximum, zs)
    return top, tree(jnp.add, [jnp.exp2(z - top) for z in zs])


def lse_lead(parts_ref):
    top, total = lse_list([parts_ref[k] for k in range(parts_ref.shape[0])])
    return top + jnp.log2(total)


def send(part_ref, out_ref):
    part = part_ref[...]
    for k in range(out_ref.shape[0]):
        out_ref[k] = part


def columns_kernel(val_hbm, columns_ref, val_ref, sem):
    copy = pltpu.make_async_copy(val_hbm, val_ref, sem)
    copy.start()
    copy.wait()
    for quarter in range(4):
        first = member(quarter, 0, 0)
        for block in range(NB):
            piece = val_ref[:, pl.ds((quarter * NB + block) * T, T)]
            for feature in range(2):
                columns_ref[first, pl.ds(feature * NB + block, 1), :] = piece[feature : feature + 1]
        whole = columns_ref[first]
        for z in range(4):
            for y in range(4):
                if z or y:
                    columns_ref[member(quarter, z, y)] = whole


def rows_kernel(index_hbm, labels_hbm, pool_hbm, rows_ref, index_ref, labels_ref, pool_ref, column_ref, sems):
    moves = [(index_hbm, index_ref), (labels_hbm, labels_ref), (pool_hbm, pool_ref)]
    copies = [pltpu.make_async_copy(a, b, sems.at[k]) for k, (a, b) in enumerate(moves)]
    for copy in copies:
        copy.start()
    for copy in copies:
        copy.wait()

    def step(i, carry):
        for j in range(16):
            at = i * 16 + j
            place = index_ref[at]
            rows_ref[pl.ds(at, 1), :] = pool_ref[pl.ds(place, 1), :]
            column_ref[pl.ds(at, 1), :] = jnp.full((1, T), labels_ref[place].astype(F32), F32)
        return carry

    lax.fori_loop(0, OWN // 16, step, 0)
    flat = [column_ref[k * T : (k + 1) * T, :].T[0:1] for k in range(OWN // T)]
    rows_ref[OWN : OWN + 8, :] = jnp.concatenate(flat + [jnp.zeros((8 - OWN // T, T), F32)], axis=0)


def labels_kernel(quarter_ref, labels_ref, class_ref, out_ref):
    classes = class_ref.shape[0]
    own = labels_ref[pl.ds(pl.multiple_of(quarter_ref[0] * NB, NB), NB), :]
    kinds = class_ref[...] * (-SCALE)
    for block in range(NB):
        onehot = (lax.broadcasted_iota(jnp.int32, (classes, T), 0) == own[block : block + 1]).astype(F32)
        mapped = jnp.dot(kinds, onehot, precision=lax.Precision.HIGHEST, preferred_element_type=F32)
        mapped = jnp.concatenate([mapped, jnp.zeros((16 - classes, T), F32)], axis=0)
        hi, mid, low = split3(mapped)
        filled = jnp.concatenate([hi, mid, low, jnp.zeros((T - 48, T), BF16)], axis=0)
        out_ref[:, block * T : (block + 1) * T] = filled


def rows_block(load, piece_ref):
    for piece in range(T // 32):
        top, total = lse_list([load(block, piece * 32) for block in range(NB)])
        piece_ref[piece * 32 : (piece + 1) * 32, :] = top + jnp.log2(total)
    flat = piece_ref[...].T
    top = jnp.max(flat, axis=0, keepdims=True)
    return top + jnp.log2(jnp.sum(jnp.exp2(flat - top), axis=0, keepdims=True))


def left_rows(rows_ref):
    x = rows_ref[0:OWN, :]
    squares = jnp.sum(x * x, axis=1, keepdims=True) * (-SCALE / T)
    hi, mid, low = split3(x * (2.0 * SCALE / T))
    lane = lax.broadcasted_iota(jnp.int32, (OWN, T), 1)
    flat = [jnp.broadcast_to(rows_ref[OWN + k : OWN + k + 1, :], (T, T)).T for k in range(OWN // T)]
    label = jnp.concatenate(flat, axis=0).astype(jnp.int32)
    ext = jnp.where((lane % 16 == label) & (lane < 48), 1.0, 0.0).astype(BF16)
    return jnp.concatenate([hi, hi, mid, hi, low, mid, ext], axis=1), squares


def group_costs(left, b, squares_v, cost_ref, start):
    a, squares = left
    cost_ref[start : start + OWN, :] = jnp.dot(a, b, preferred_element_type=F32) + squares + squares_v


def group_lse(cost_ref, start, place, part_ref, piece_ref):
    for half in range(OWN // T):

        def load(block, row):
            first = start + half * T + row
            return cost_ref[first : first + 32, block * T : (block + 1) * T]

        part_ref[pl.ds(place + half, 1), :] = rows_block(load, piece_ref.at[half])


def first_costs_kernel(rows_ref, rows3_ref, val_ref, kinds_ref, quarter_ref, cost_ref, part_ref, b_ref, squares_ref, piece_ref):
    for block in range(NB):
        lanes = slice(block * T, (block + 1) * T)
        y = in_order(val_ref[pl.ds(block, T, stride=NB), :])
        hi, mid, low = split3(y)
        for k, part in enumerate((hi, mid, hi, low, hi, mid)):
            b_ref[k * T : (k + 1) * T, lanes] = part
        squares_ref[:, lanes] = jnp.broadcast_to(jnp.sum(y * y, axis=0, keepdims=True) * (-SCALE / T), (8, T))
    b_ref[6 * T : 7 * T, :] = kinds_ref[...]
    tile_costs((rows_ref, rows3_ref), (0, 3), quarter_ref[0], b_ref, squares_ref, cost_ref, part_ref, piece_ref)


def other_costs_kernel(
    rows1_ref, rows2_ref, b_ref, squares_ref, quarter_ref, part_ref, cost_ref, out_ref, full_ref, piece_ref
):
    full_ref[...] = part_ref[...]
    tile_costs((rows1_ref, rows2_ref), (1, 2), quarter_ref[0], b_ref, squares_ref, cost_ref, full_ref, piece_ref)
    send(full_ref, out_ref)


def tile_costs(groups, aparts, quarter, b_ref, squares_ref, cost_ref, part_ref, piece_ref):
    for k, rows_ref in enumerate(groups):
        group_costs(left_rows(rows_ref), b_ref[...], squares_ref[0:1, :], cost_ref, k * OWN)
    for k, apart in enumerate(aparts):
        group_lse(cost_ref, k * OWN, (quarter ^ apart) * 2, part_ref, piece_ref.at[k])


def tile_rows(first_ref, rest_ref, s):
    return (first_ref, s * T) if s < NB // 2 else (rest_ref, (s - NB // 2) * T)


def place(quarter, s):
    return (quarter ^ (0, 3, 1, 2)[s // 2]) * 2 + s % 2


def rows_step_kernel(parts_ref, first_ref, rest_ref, quarter_ref, out_ref, piece_ref, part_ref):
    g = -15.0 - lse_lead(parts_ref)
    wide = [jnp.broadcast_to(g[block : block + 1], (32, T)) for block in range(NB)]
    for s in range(NB):
        cost_ref, start = tile_rows(first_ref, rest_ref, s)

        def load(block, row):
            return cost_ref[start + row : start + row + 32, block * T : (block + 1) * T] + wide[block]

        part_ref[pl.ds(place(quarter_ref[0], s), 1), :] = rows_block(load, piece_ref.at[s])
    send(part_ref, out_ref)


def columns_lse(f_ref, first_ref, rest_ref, quarter, wide_ref, part_ref):
    for s in range(NB):
        row = f_ref[pl.ds(place(quarter, s), 1), :]
        wide_ref[s * T : (s + 1) * T, :] = jnp.broadcast_to(row, (T, T)).T
    for block in range(NB):
        lanes = slice(block * T, (block + 1) * T)
        tops, totals = [], []
        for chunk in range(SIDE // 64):
            cost_ref, first = tile_rows(first_ref, rest_ref, chunk // 2)
            first = first + chunk % 2 * 64
            zs = []
            for j in range(0, 64, 8):
                at = chunk * 64 + j
                zs.append(cost_ref[first + j : first + j + 8, lanes] + wide_ref[at : at + 8, :])
            top, total = lse_list(zs)
            tops.append(top)
            totals.append(total)
        best = jnp.max(tree(jnp.maximum, tops), axis=0, keepdims=True)
        total = tree(jnp.add, [total * jnp.exp2(top - best) for top, total in zip(tops, totals)])
        part_ref[block : block + 1, :] = best + jnp.log2(jnp.sum(total, axis=0, keepdims=True))


def columns_step_kernel(parts_ref, first_ref, rest_ref, quarter_ref, out_ref, wide_ref, part_ref, f_ref):
    f_ref[...] = -14.0 - lse_lead(parts_ref)
    columns_lse(f_ref, first_ref, rest_ref, quarter_ref[0], wide_ref, part_ref)
    send(part_ref, out_ref)


def last_columns_kernel(parts_ref, first_ref, rest_ref, quarter_ref, out_ref, f_ref, wide_ref, part_ref, row_ref):
    f = -14.0 - lse_lead(parts_ref)
    f_ref[...] = f
    columns_lse(f_ref, first_ref, rest_ref, quarter_ref[0], wide_ref, part_ref)
    for block in range(NB):
        row_ref[:, block * T : (block + 1) * T] = part_ref[block : block + 1, :]
    row_ref[:, SIDE : SIDE + T] = jnp.sum(f, axis=0, keepdims=True)
    send(row_ref, out_ref)


def finish_kernel(parts_ref, f_ref, quarter_ref, value_ref, potential_ref):
    total = tree(jnp.add, [parts_ref[k, :, SIDE : SIDE + T] for k in range(parts_ref.shape[0])])
    mean = jnp.sum(total) * (0.25 / 16384.0)
    value_ref[...] = (f_ref[pl.ds(quarter_ref[0] * 2, 2), :] - mean) * BACK
    for quarter in range(4):
        parts = [parts_ref[member(quarter, z, y), :, 0:SIDE] for z in range(4) for y in range(4)]
        top, whole = lse_list(parts)
        potential_ref[quarter] = (-15.0 - (top + jnp.log2(whole))) * BACK


SPEC = pl.BlockSpec(memory_space=pltpu.VMEM)
SCALARS = pl.BlockSpec(memory_space=pltpu.SMEM)
FAR = pl.BlockSpec(memory_space=pltpu.HBM)


def vmem(shape, dtype=F32):
    return pltpu.VMEM(shape, dtype)


def far(x):
    return pltpu.with_memory_space_constraint(x, pltpu.HBM)


def shape(dims, dtype=F32):
    return jax.ShapeDtypeStruct(dims, dtype)


def call(kernel, out, ins, scratch=()):
    return pl.pallas_call(
        kernel,
        out_shape=out,
        in_specs=ins,
        out_specs=[SPEC] * len(out),
        scratch_shapes=list(scratch),
        compiler_params=PARAMS,
    )


def local(pool, window_index, pool_labels, val_embed, val_labels, class_cost):
    quarter = lax.axis_index(QUAD).astype(jnp.int32).reshape(1)
    (columns,) = call(
        columns_kernel, [shape((64, 16, T))], [FAR], [vmem((2, 4096)), pltpu.SemaphoreType.DMA(())]
    )(far(val_embed.T))
    columns, window_index = lax.optimization_barrier((columns, window_index))
    (rows,) = call(
        rows_kernel,
        [shape((OWN + 8, T))],
        [FAR] * 3,
        [
            pltpu.SMEM(window_index.shape, jnp.int32),
            pltpu.SMEM(pool_labels.shape, jnp.int32),
            vmem(pool.shape),
            vmem((OWN, T)),
            pltpu.SemaphoreType.DMA((3,)),
        ],
    )(far(window_index), far(pool_labels), far(pool))
    columns = lax.all_to_all(columns, ROW, 0, 0, axis_index_groups=ROW_ORDER)
    others = [lax.ppermute(rows, QUAD, [(i, i ^ apart) for i in range(4)]) for apart in (1, 2, 3)]
    rows, val_labels, class_cost = lax.optimization_barrier((rows, val_labels, class_cost))
    (kinds,) = call(labels_kernel, [shape((T, SIDE), BF16)], [SCALARS, SPEC, SPEC])(
        quarter, val_labels.reshape(32, T), class_cost
    )
    part, piece, wide = vmem((NB, T)), vmem((NB, T, T)), vmem((SIDE, T))
    first, part_first, b, squares = call(
        first_costs_kernel,
        [shape((2 * OWN, SIDE)), shape((NB, T)), shape((7 * T, SIDE), BF16), shape((8, SIDE))],
        [SPEC] * 4 + [SCALARS],
        [vmem((2, 2, T, T))],
    )(rows, others[2], columns.reshape(SIDE, T), kinds, quarter)
    rest, parts = call(
        other_costs_kernel,
        [shape((2 * OWN, SIDE)), shape((32, NB, T))],
        [SPEC] * 4 + [SCALARS, SPEC],
        [part, vmem((2, 2, T, T))],
    )(*others[:2], b, squares, quarter, part_first)
    step = [SPEC] * 3 + [SCALARS]
    parts = lax.all_to_all(parts, ALONG, 0, 0, axis_index_groups=ALONG_ORDER)
    (parts,) = call(columns_step_kernel, [shape((16, NB, T))], step, [wide, part, part])(parts, first, rest, quarter)
    parts = lax.all_to_all(parts, ACROSS, 0, 0, axis_index_groups=ACROSS_ORDER)
    (parts,) = call(rows_step_kernel, [shape((32, NB, T))], step, [piece, part])(parts, first, rest, quarter)
    parts = lax.all_to_all(parts, ALONG, 0, 0, axis_index_groups=ALONG_ORDER)
    parts, f = call(
        last_columns_kernel, [shape((64, 1, SIDE + T)), shape((NB, T))], step, [wide, part, vmem((1, SIDE + T))]
    )(parts, first, rest, quarter)
    parts = lax.all_to_all(parts, ROW, 0, 0, axis_index_groups=ROW_ORDER)
    value, potential = call(finish_kernel, [shape((2, T)), shape((4, 1, SIDE))], [SPEC, SPEC, SCALARS])(parts, f, quarter)
    return value.reshape(256), potential.reshape(4096)


def solution(mesh):
    fine = Mesh(mesh.devices.reshape(2, 2, 2, 2, 2, 2, 4, 2), ROW + COL)
    placed = (P(ROW, None), P(ROW), P(ROW), P(COL, ROW), P(COL), P())
    return jax.shard_map(local, mesh=fine, in_specs=placed, out_specs=(P(ROW), P(COL)), check_vma=False)
```

```python
import math

import jax
import jax.numpy as jnp
from jax import lax
from jax.experimental import pallas as pl
from jax.experimental.pallas import tpu as pltpu
from jax.sharding import Mesh
from jax.sharding import PartitionSpec as P

EPSILON = 0.02
SCALE = 1.0 / (EPSILON * math.log(2.0))
BACK = EPSILON * math.log(2.0)

ROW = ("z2", "z1", "z0", "y2", "y1", "y0")
COL = ("x", "core")
QUAD = ("z0", "y0")
ACROSS = ("z2", "z1", "y2", "y1")
ALONG = QUAD + COL

FIRST = (4, 4)


def turned(z_size, y_size, z_first, y_first):
    return [[(z + z_first) % z_size * y_size + (y + y_first) % y_size for z in range(z_size) for y in range(y_size)]]


ROW_ORDER = turned(8, 8, *FIRST)
ACROSS_ORDER = turned(4, 4, FIRST[0] // 2, FIRST[1] // 2)
ALONG_ORDER = [[(quarter ^ 3) * 8 + (x + 2) % 4 * 2 + (1 - core) for quarter in range(4) for x in range(4) for core in range(2)]]

T = 128
NB = 8
SIDE = NB * T
OWN = 256
PARAMS = pltpu.CompilerParams(vmem_limit_bytes=20 * 1024 * 1024)
F32 = jnp.float32
BF16 = jnp.bfloat16


def split3(x):
    hi = x.astype(BF16)
    rest = x - hi.astype(F32)
    mid = rest.astype(BF16)
    low = (rest - mid.astype(F32)).astype(BF16)
    return hi, mid, low


def member(quarter, z, y):
    return ((z * 2 + quarter // 2) * 4 + y) * 2 + quarter % 2


def in_order(y):
    places = [(z - FIRST[0]) % 8 * 2 + (half - FIRST[1] // 4) % 2 for z in range(8) for half in range(2)]
    return jnp.concatenate([y[8 * place : 8 * place + 8] for place in places], axis=0)


def tree(op, xs):
    xs = list(xs)
    while len(xs) > 1:
        xs = [op(*xs[i : i + 2]) if i + 1 < len(xs) else xs[i] for i in range(0, len(xs), 2)]
    return xs[0]


def lse_list(zs):
    top = tree(jnp.maximum, zs)
    return top, tree(jnp.add, [jnp.exp2(z - top) for z in zs])


def lse_lead(parts_ref):
    top, total = lse_list([parts_ref[k] for k in range(parts_ref.shape[0])])
    return top + jnp.log2(total)


def send(part_ref, out_ref):
    part = part_ref[...]
    for k in range(out_ref.shape[0]):
        out_ref[k] = part


def columns_kernel(val_hbm, columns_ref, val_ref, sem):
    copy = pltpu.make_async_copy(val_hbm, val_ref, sem)
    copy.start()
    copy.wait()
    for quarter in range(4):
        first = member(quarter, 0, 0)
        for block in range(NB):
            piece = val_ref[:, pl.ds((quarter * NB + block) * T, T)]
            for feature in range(2):
                columns_ref[first, pl.ds(feature * NB + block, 1), :] = piece[feature : feature + 1]
        whole = columns_ref[first]
        for z in range(4):
            for y in range(4):
                if z or y:
                    columns_ref[member(quarter, z, y)] = whole


def rows_kernel(index_hbm, labels_hbm, pool_hbm, rows_ref, index_ref, labels_ref, pool_ref, column_ref, sems):
    moves = [(index_hbm, index_ref), (labels_hbm, labels_ref), (pool_hbm, pool_ref)]
    copies = [pltpu.make_async_copy(a, b, sems.at[k]) for k, (a, b) in enumerate(moves)]
    for copy in copies:
        copy.start()
    for copy in copies:
        copy.wait()

    def step(i, carry):
        for j in range(16):
            at = i * 16 + j
            place = index_ref[at]
            rows_ref[pl.ds(at, 1), :] = pool_ref[pl.ds(place, 1), :]
            column_ref[pl.ds(at, 1), :] = jnp.full((1, T), labels_ref[place].astype(F32), F32)
        return carry

    lax.fori_loop(0, OWN // 16, step, 0)
    flat = [column_ref[k * T : (k + 1) * T, :].T[0:1] for k in range(OWN // T)]
    rows_ref[OWN : OWN + 8, :] = jnp.concatenate(flat + [jnp.zeros((8 - OWN // T, T), F32)], axis=0)


def labels_kernel(quarter_ref, labels_ref, class_ref, out_ref):
    classes = class_ref.shape[0]
    own = labels_ref[pl.ds(pl.multiple_of(quarter_ref[0] * NB, NB), NB), :]
    kinds = class_ref[...] * (-SCALE)
    for block in range(NB):
        onehot = (lax.broadcasted_iota(jnp.int32, (classes, T), 0) == own[block : block + 1]).astype(F32)
        mapped = jnp.dot(kinds, onehot, precision=lax.Precision.HIGHEST, preferred_element_type=F32)
        mapped = jnp.concatenate([mapped, jnp.zeros((16 - classes, T), F32)], axis=0)
        hi, mid, low = split3(mapped)
        filled = jnp.concatenate([hi, mid, low, jnp.zeros((T - 48, T), BF16)], axis=0)
        out_ref[:, block * T : (block + 1) * T] = filled


def rows_block(load, piece_ref):
    for piece in range(T // 32):
        top, total = lse_list([load(block, piece * 32) for block in range(NB)])
        piece_ref[piece * 32 : (piece + 1) * 32, :] = top + jnp.log2(total)
    flat = piece_ref[...].T
    top = jnp.max(flat, axis=0, keepdims=True)
    return top + jnp.log2(jnp.sum(jnp.exp2(flat - top), axis=0, keepdims=True))


def left_rows(rows_ref):
    x = rows_ref[0:OWN, :]
    squares = jnp.sum(x * x, axis=1, keepdims=True) * (-SCALE / T)
    hi, mid, low = split3(x * (2.0 * SCALE / T))
    lane = lax.broadcasted_iota(jnp.int32, (OWN, T), 1)
    flat = [jnp.broadcast_to(rows_ref[OWN + k : OWN + k + 1, :], (T, T)).T for k in range(OWN // T)]
    label = jnp.concatenate(flat, axis=0).astype(jnp.int32)
    ext = jnp.where((lane % 16 == label) & (lane < 48), 1.0, 0.0).astype(BF16)
    return jnp.concatenate([hi, hi, mid, hi, low, mid, ext], axis=1), squares


def left_kernel(rows_ref, rows1_ref, left_ref, squares_ref):
    for k, ref in enumerate((rows_ref, rows1_ref)):
        a, squares = left_rows(ref)
        left_ref[k * OWN : (k + 1) * OWN, :] = a
        squares_ref[k * OWN : (k + 1) * OWN, :] = jnp.broadcast_to(squares, (OWN, T))


def group_costs(left, b, squares_v, cost_ref, start):
    a, squares = left
    cost_ref[start : start + OWN, :] = jnp.dot(a, b, preferred_element_type=F32) + squares + squares_v


def group_lse(cost_ref, start, place, part_ref, piece_ref):
    for half in range(OWN // T):

        def load(block, row):
            first = start + half * T + row
            return cost_ref[first : first + 32, block * T : (block + 1) * T]

        part_ref[pl.ds(place + half, 1), :] = rows_block(load, piece_ref.at[half])


def first_costs_kernel(left_ref, left_squares_ref, val_ref, kinds_ref, quarter_ref, cost_ref, part_ref, b_ref, squares_ref, piece_ref):
    for block in range(NB):
        lanes = slice(block * T, (block + 1) * T)
        y = in_order(val_ref[pl.ds(block, T, stride=NB), :])
        hi, mid, low = split3(y)
        for k, part in enumerate((hi, mid, hi, low, hi, mid)):
            b_ref[k * T : (k + 1) * T, lanes] = part
        squares_ref[:, lanes] = jnp.broadcast_to(jnp.sum(y * y, axis=0, keepdims=True) * (-SCALE / T), (8, T))
    b_ref[6 * T : 7 * T, :] = kinds_ref[...]
    lefts = [(left_ref[rows, :], left_squares_ref[rows, 0:1]) for rows in (slice(0, OWN), slice(OWN, 2 * OWN))]
    tile_costs(lefts, (0, 1), quarter_ref[0], b_ref, squares_ref, cost_ref, part_ref, piece_ref)


def other_costs_kernel(
    rows2_ref, rows3_ref, b_ref, squares_ref, quarter_ref, part_ref, cost_ref, out_ref, full_ref, piece_ref
):
    full_ref[...] = part_ref[...]
    tile_costs((left_rows(rows2_ref), left_rows(rows3_ref)), (2, 3), quarter_ref[0], b_ref, squares_ref, cost_ref, full_ref, piece_ref)
    send(full_ref, out_ref)


def tile_costs(lefts, aparts, quarter, b_ref, squares_ref, cost_ref, part_ref, piece_ref):
    for k, left in enumerate(lefts):
        group_costs(left, b_ref[...], squares_ref[0:1, :], cost_ref, k * OWN)
    for k, apart in enumerate(aparts):
        group_lse(cost_ref, k * OWN, (quarter ^ apart) * 2, part_ref, piece_ref.at[k])


def tile_rows(first_ref, rest_ref, s):
    return (first_ref, s * T) if s < NB // 2 else (rest_ref, (s - NB // 2) * T)


def place(quarter, s):
    return (quarter ^ (s // 2)) * 2 + s % 2


def rows_step_kernel(parts_ref, first_ref, rest_ref, quarter_ref, out_ref, piece_ref, part_ref):
    g = -15.0 - lse_lead(parts_ref)
    wide = [jnp.broadcast_to(g[block : block + 1], (32, T)) for block in range(NB)]
    for s in range(NB):
        cost_ref, start = tile_rows(first_ref, rest_ref, s)

        def load(block, row):
            return cost_ref[start + row : start + row + 32, block * T : (block + 1) * T] + wide[block]

        part_ref[pl.ds(place(quarter_ref[0], s), 1), :] = rows_block(load, piece_ref.at[s])
    send(part_ref, out_ref)


def columns_lse(f_ref, first_ref, rest_ref, quarter, wide_ref, part_ref):
    for s in range(NB):
        row = f_ref[pl.ds(place(quarter, s), 1), :]
        wide_ref[s * T : (s + 1) * T, :] = jnp.broadcast_to(row, (T, T)).T
    for block in range(NB):
        lanes = slice(block * T, (block + 1) * T)
        tops, totals = [], []
        for chunk in range(SIDE // 64):
            cost_ref, first = tile_rows(first_ref, rest_ref, chunk // 2)
            first = first + chunk % 2 * 64
            zs = []
            for j in range(0, 64, 8):
                at = chunk * 64 + j
                zs.append(cost_ref[first + j : first + j + 8, lanes] + wide_ref[at : at + 8, :])
            top, total = lse_list(zs)
            tops.append(top)
            totals.append(total)
        best = jnp.max(tree(jnp.maximum, tops), axis=0, keepdims=True)
        total = tree(jnp.add, [total * jnp.exp2(top - best) for top, total in zip(tops, totals)])
        part_ref[block : block + 1, :] = best + jnp.log2(jnp.sum(total, axis=0, keepdims=True))


def columns_step_kernel(parts_ref, first_ref, rest_ref, quarter_ref, out_ref, wide_ref, part_ref, f_ref):
    f_ref[...] = -14.0 - lse_lead(parts_ref)
    columns_lse(f_ref, first_ref, rest_ref, quarter_ref[0], wide_ref, part_ref)
    send(part_ref, out_ref)


def last_columns_kernel(parts_ref, first_ref, rest_ref, quarter_ref, out_ref, f_ref, wide_ref, part_ref, row_ref):
    f = -14.0 - lse_lead(parts_ref)
    f_ref[...] = f
    columns_lse(f_ref, first_ref, rest_ref, quarter_ref[0], wide_ref, part_ref)
    for block in range(NB):
        row_ref[:, block * T : (block + 1) * T] = part_ref[block : block + 1, :]
    row_ref[:, SIDE : SIDE + T] = jnp.sum(f, axis=0, keepdims=True)
    send(row_ref, out_ref)


def finish_kernel(parts_ref, f_ref, quarter_ref, value_ref, potential_ref):
    total = tree(jnp.add, [parts_ref[k, :, SIDE : SIDE + T] for k in range(parts_ref.shape[0])])
    mean = jnp.sum(total) * (0.25 / 16384.0)
    value_ref[...] = (f_ref[pl.ds(quarter_ref[0] * 2, 2), :] - mean) * BACK
    for quarter in range(4):
        parts = [parts_ref[member(quarter, z, y), :, 0:SIDE] for z in range(4) for y in range(4)]
        top, whole = lse_list(parts)
        potential_ref[quarter] = (-15.0 - (top + jnp.log2(whole))) * BACK


SPEC = pl.BlockSpec(memory_space=pltpu.VMEM)
SCALARS = pl.BlockSpec(memory_space=pltpu.SMEM)
FAR = pl.BlockSpec(memory_space=pltpu.HBM)


def vmem(shape, dtype=F32):
    return pltpu.VMEM(shape, dtype)


def far(x):
    return pltpu.with_memory_space_constraint(x, pltpu.HBM)


def shape(dims, dtype=F32):
    return jax.ShapeDtypeStruct(dims, dtype)


def call(kernel, out, ins, scratch=()):
    return pl.pallas_call(
        kernel,
        out_shape=out,
        in_specs=ins,
        out_specs=[SPEC] * len(out),
        scratch_shapes=list(scratch),
        compiler_params=PARAMS,
    )


def local(pool, window_index, pool_labels, val_embed, val_labels, class_cost):
    quarter = lax.axis_index(QUAD).astype(jnp.int32).reshape(1)
    (columns,) = call(
        columns_kernel, [shape((64, 16, T))], [FAR], [vmem((2, 4096)), pltpu.SemaphoreType.DMA(())]
    )(far(val_embed.T))
    columns, window_index = lax.optimization_barrier((columns, window_index))
    (rows,) = call(
        rows_kernel,
        [shape((OWN + 8, T))],
        [FAR] * 3,
        [
            pltpu.SMEM(window_index.shape, jnp.int32),
            pltpu.SMEM(pool_labels.shape, jnp.int32),
            vmem(pool.shape),
            vmem((OWN, T)),
            pltpu.SemaphoreType.DMA((3,)),
        ],
    )(far(window_index), far(pool_labels), far(pool))
    columns = lax.all_to_all(columns, ROW, 0, 0, axis_index_groups=ROW_ORDER)
    others = {apart: lax.ppermute(rows, QUAD, [(i, i ^ apart) for i in range(4)]) for apart in (2, 3, 1)}
    rows, val_labels, class_cost = lax.optimization_barrier((rows, val_labels, class_cost))
    (kinds,) = call(labels_kernel, [shape((T, SIDE), BF16)], [SCALARS, SPEC, SPEC])(
        quarter, val_labels.reshape(32, T), class_cost
    )
    part, piece, wide = vmem((NB, T)), vmem((NB, T, T)), vmem((SIDE, T))
    left, left_squares = call(left_kernel, [shape((2 * OWN, 7 * T), BF16), shape((2 * OWN, T))], [SPEC] * 2)(rows, others[1])
    first, part_first, b, squares = call(
        first_costs_kernel,
        [shape((2 * OWN, SIDE)), shape((NB, T)), shape((7 * T, SIDE), BF16), shape((8, SIDE))],
        [SPEC] * 4 + [SCALARS],
        [vmem((2, 2, T, T))],
    )(left, left_squares, columns.reshape(SIDE, T), kinds, quarter)
    rest, parts = call(
        other_costs_kernel,
        [shape((2 * OWN, SIDE)), shape((32, NB, T))],
        [SPEC] * 4 + [SCALARS, SPEC],
        [part, vmem((2, 2, T, T))],
    )(others[2], others[3], b, squares, quarter, part_first)
    step = [SPEC] * 3 + [SCALARS]
    parts = lax.all_to_all(parts, ALONG, 0, 0, axis_index_groups=ALONG_ORDER)
    (parts,) = call(columns_step_kernel, [shape((16, NB, T))], step, [wide, part, part])(parts, first, rest, quarter)
    parts = lax.all_to_all(parts, ACROSS, 0, 0, axis_index_groups=ACROSS_ORDER)
    (parts,) = call(rows_step_kernel, [shape((32, NB, T))], step, [piece, part])(parts, first, rest, quarter)
    parts = lax.all_to_all(parts, ALONG, 0, 0, axis_index_groups=ALONG_ORDER)
    parts, f = call(
        last_columns_kernel, [shape((64, 1, SIDE + T)), shape((NB, T))], step, [wide, part, vmem((1, SIDE + T))]
    )(parts, first, rest, quarter)
    parts = lax.all_to_all(parts, ROW, 0, 0, axis_index_groups=ROW_ORDER)
    value, potential = call(finish_kernel, [shape((2, T)), shape((4, 1, SIDE))], [SPEC, SPEC, SCALARS])(parts, f, quarter)
    return value.reshape(256), potential.reshape(4096)


def solution(mesh):
    fine = Mesh(mesh.devices.reshape(2, 2, 2, 2, 2, 2, 4, 2), ROW + COL)
    placed = (P(ROW, None), P(ROW), P(ROW), P(COL, ROW), P(COL), P())
    return jax.shard_map(local, mesh=fine, in_specs=placed, out_specs=(P(ROW), P(COL)), check_vma=False)
```

```python
import math

import jax
import jax.numpy as jnp
from jax import lax
from jax.experimental import pallas as pl
from jax.experimental.pallas import tpu as pltpu
from jax.sharding import Mesh
from jax.sharding import PartitionSpec as P

EPSILON = 0.02
SCALE = 1.0 / (EPSILON * math.log(2.0))
BACK = EPSILON * math.log(2.0)

ROW = ("z2", "z1", "z0", "y2", "y1", "y0")
COL = ("x", "core")
QUAD = ("z0", "y0")
ACROSS = ("z2", "z1", "y2", "y1")
ALONG = QUAD + COL

FIRST = (4, 4)


def turned(z_size, y_size, z_first, y_first):
    return [[(z + z_first) % z_size * y_size + (y + y_first) % y_size for z in range(z_size) for y in range(y_size)]]


ROW_ORDER = turned(8, 8, *FIRST)
ACROSS_ORDER = turned(4, 4, FIRST[0] // 2, FIRST[1] // 2)
ALONG_ORDER = [[(quarter ^ 3) * 8 + (x + 2) % 4 * 2 + (1 - core) for quarter in range(4) for x in range(4) for core in range(2)]]

T = 128
NB = 8
SIDE = NB * T
OWN = 256
PARAMS = pltpu.CompilerParams(vmem_limit_bytes=20 * 1024 * 1024)
F32 = jnp.float32
BF16 = jnp.bfloat16


def split3(x):
    hi = x.astype(BF16)
    rest = x - hi.astype(F32)
    mid = rest.astype(BF16)
    low = (rest - mid.astype(F32)).astype(BF16)
    return hi, mid, low


def member(quarter, z, y):
    return ((z * 2 + quarter // 2) * 4 + y) * 2 + quarter % 2


def in_order(y):
    places = [(z - FIRST[0]) % 8 * 2 + (half - FIRST[1] // 4) % 2 for z in range(8) for half in range(2)]
    return jnp.concatenate([y[8 * place : 8 * place + 8] for place in places], axis=0)


def tree(op, xs):
    xs = list(xs)
    while len(xs) > 1:
        xs = [op(*xs[i : i + 2]) if i + 1 < len(xs) else xs[i] for i in range(0, len(xs), 2)]
    return xs[0]


def lse_list(zs):
    top = tree(jnp.maximum, zs)
    return top, tree(jnp.add, [jnp.exp2(z - top) for z in zs])


def lse_lead(parts_ref):
    top, total = lse_list([parts_ref[k] for k in range(parts_ref.shape[0])])
    return top + jnp.log2(total)


def send(part_ref, out_ref):
    part = part_ref[...]
    for k in range(out_ref.shape[0]):
        out_ref[k] = part


def columns_kernel(val_hbm, columns_ref, val_ref, sem):
    copy = pltpu.make_async_copy(val_hbm, val_ref, sem)
    copy.start()
    copy.wait()
    for quarter in range(4):
        first = member(quarter, 0, 0)
        for block in range(NB):
            piece = val_ref[:, pl.ds((quarter * NB + block) * T, T)]
            for feature in range(2):
                columns_ref[first, pl.ds(feature * NB + block, 1), :] = piece[feature : feature + 1]
        whole = columns_ref[first]
        for z in range(4):
            for y in range(4):
                if z or y:
                    columns_ref[member(quarter, z, y)] = whole


def rows_kernel(index_hbm, labels_hbm, pool_hbm, rows_ref, index_ref, labels_ref, pool_ref, column_ref, sems):
    moves = [(index_hbm, index_ref), (labels_hbm, labels_ref), (pool_hbm, pool_ref)]
    copies = [pltpu.make_async_copy(a, b, sems.at[k]) for k, (a, b) in enumerate(moves)]
    for copy in copies:
        copy.start()
    for copy in copies:
        copy.wait()

    def step(i, carry):
        for j in range(16):
            at = i * 16 + j
            place = index_ref[at]
            rows_ref[pl.ds(at, 1), :] = pool_ref[pl.ds(place, 1), :]
            column_ref[pl.ds(at, 1), :] = jnp.full((1, T), labels_ref[place].astype(F32), F32)
        return carry

    lax.fori_loop(0, OWN // 16, step, 0)
    flat = [column_ref[k * T : (k + 1) * T, :].T[0:1] for k in range(OWN // T)]
    rows_ref[OWN : OWN + 8, :] = jnp.concatenate(flat + [jnp.zeros((8 - OWN // T, T), F32)], axis=0)


def labels_kernel(quarter_ref, labels_ref, class_ref, out_ref):
    classes = class_ref.shape[0]
    own = labels_ref[pl.ds(pl.multiple_of(quarter_ref[0] * NB, NB), NB), :]
    kinds = class_ref[...] * (-SCALE)
    ones = jnp.where(lax.broadcasted_iota(jnp.int32, (16, T), 0) < 3, 1.0, 0.0).astype(BF16)
    for block in range(NB):
        onehot = (lax.broadcasted_iota(jnp.int32, (classes, T), 0) == own[block : block + 1]).astype(F32)
        mapped = jnp.dot(kinds, onehot, precision=lax.Precision.HIGHEST, preferred_element_type=F32)
        mapped = jnp.concatenate([mapped, jnp.zeros((16 - classes, T), F32)], axis=0)
        hi, mid, low = split3(mapped)
        filled = jnp.concatenate([hi, mid, low, ones, jnp.zeros((T - 64, T), BF16)], axis=0)
        out_ref[:, block * T : (block + 1) * T] = filled


def rows_block(load, piece_ref):
    for piece in range(T // 32):
        top, total = lse_list([load(block, piece * 32) for block in range(NB)])
        piece_ref[piece * 32 : (piece + 1) * 32, :] = top + jnp.log2(total)
    flat = piece_ref[...].T
    top = jnp.max(flat, axis=0, keepdims=True)
    return top + jnp.log2(jnp.sum(jnp.exp2(flat - top), axis=0, keepdims=True))


def left_rows(rows_ref):
    x = rows_ref[0:OWN, :]
    squares = jnp.sum(x * x, axis=1, keepdims=True) * (-SCALE / T)
    hi, mid, low = split3(x * (2.0 * SCALE / T))
    lane = lax.broadcasted_iota(jnp.int32, (OWN, T), 1)
    flat = [jnp.broadcast_to(rows_ref[OWN + k : OWN + k + 1, :], (T, T)).T for k in range(OWN // T)]
    label = jnp.concatenate(flat, axis=0).astype(jnp.int32)
    ext = jnp.where((lane % 16 == label) | (lane >= 51), 1.0, 0.0)
    for k, part in enumerate(split3(squares)):
        ext = jnp.where(lane == 48 + k, part.astype(F32), ext)
    ext = jnp.where(lane < 54, ext, 0.0).astype(BF16)
    return jnp.concatenate([hi, hi, mid, hi, low, mid, ext], axis=1)


def left_kernel(rows_ref, rows1_ref, left_ref):
    for k, ref in enumerate((rows_ref, rows1_ref)):
        left_ref[k * OWN : (k + 1) * OWN, :] = left_rows(ref)


def group_costs(left, b, cost_ref, start):
    cost_ref[start : start + OWN, :] = jnp.dot(left, b, preferred_element_type=F32)


def group_lse(cost_ref, start, place, part_ref, piece_ref):
    for half in range(OWN // T):

        def load(block, row):
            first = start + half * T + row
            return cost_ref[first : first + 32, block * T : (block + 1) * T]

        part_ref[pl.ds(place + half, 1), :] = rows_block(load, piece_ref.at[half])


def first_costs_kernel(left_ref, val_ref, kinds_ref, quarter_ref, cost_ref, part_ref, b_ref, piece_ref):
    for block in range(NB):
        lanes = slice(block * T, (block + 1) * T)
        y = in_order(val_ref[pl.ds(block, T, stride=NB), :])
        hi, mid, low = split3(y)
        for k, part in enumerate((hi, mid, hi, low, hi, mid)):
            b_ref[k * T : (k + 1) * T, lanes] = part
        ext = kinds_ref[48:64, lanes].astype(F32)
        sub = lax.broadcasted_iota(jnp.int32, (16, T), 0)
        for k, part in enumerate(split3(jnp.sum(y * y, axis=0, keepdims=True) * (-SCALE / T))):
            ext = jnp.where(sub == 3 + k, part.astype(F32), ext)
        b_ref[6 * T : 6 * T + 48, lanes] = kinds_ref[0:48, lanes]
        b_ref[6 * T + 48 : 6 * T + 64, lanes] = ext.astype(BF16)
        b_ref[6 * T + 64 : 7 * T, lanes] = kinds_ref[64:T, lanes]
    lefts = [left_ref[rows, :] for rows in (slice(0, OWN), slice(OWN, 2 * OWN))]
    tile_costs(lefts, (0, 1), quarter_ref[0], b_ref, cost_ref, part_ref, piece_ref)


def other_costs_kernel(
    rows2_ref, rows3_ref, b_ref, quarter_ref, part_ref, cost_ref, out_ref, full_ref, piece_ref
):
    full_ref[...] = part_ref[...]
    tile_costs((left_rows(rows2_ref), left_rows(rows3_ref)), (2, 3), quarter_ref[0], b_ref, cost_ref, full_ref, piece_ref)
    send(full_ref, out_ref)


def tile_costs(lefts, aparts, quarter, b_ref, cost_ref, part_ref, piece_ref):
    for k, left in enumerate(lefts):
        group_costs(left, b_ref[...], cost_ref, k * OWN)
    for k, apart in enumerate(aparts):
        group_lse(cost_ref, k * OWN, (quarter ^ apart) * 2, part_ref, piece_ref.at[k])


def tile_rows(first_ref, rest_ref, s):
    return (first_ref, s * T) if s < NB // 2 else (rest_ref, (s - NB // 2) * T)


def place(quarter, s):
    return (quarter ^ (s // 2)) * 2 + s % 2


def rows_step_kernel(parts_ref, first_ref, rest_ref, quarter_ref, out_ref, piece_ref, part_ref):
    g = -15.0 - lse_lead(parts_ref)
    wide = [jnp.broadcast_to(g[block : block + 1], (32, T)) for block in range(NB)]
    for s in range(NB):
        cost_ref, start = tile_rows(first_ref, rest_ref, s)

        def load(block, row):
            return cost_ref[start + row : start + row + 32, block * T : (block + 1) * T] + wide[block]

        part_ref[pl.ds(place(quarter_ref[0], s), 1), :] = rows_block(load, piece_ref.at[s])
    send(part_ref, out_ref)


def columns_lse(f_ref, first_ref, rest_ref, quarter, wide_ref, part_ref):
    for s in range(NB):
        row = f_ref[pl.ds(place(quarter, s), 1), :]
        wide_ref[s * T : (s + 1) * T, :] = jnp.broadcast_to(row, (T, T)).T
    for block in range(NB):
        lanes = slice(block * T, (block + 1) * T)
        tops, totals = [], []
        for chunk in range(SIDE // 64):
            cost_ref, first = tile_rows(first_ref, rest_ref, chunk // 2)
            first = first + chunk % 2 * 64
            zs = []
            for j in range(0, 64, 8):
                at = chunk * 64 + j
                zs.append(cost_ref[first + j : first + j + 8, lanes] + wide_ref[at : at + 8, :])
            top, total = lse_list(zs)
            tops.append(top)
            totals.append(total)
        best = jnp.max(tree(jnp.maximum, tops), axis=0, keepdims=True)
        total = tree(jnp.add, [total * jnp.exp2(top - best) for top, total in zip(tops, totals)])
        part_ref[block : block + 1, :] = best + jnp.log2(jnp.sum(total, axis=0, keepdims=True))


def columns_step_kernel(parts_ref, first_ref, rest_ref, quarter_ref, out_ref, wide_ref, part_ref, f_ref):
    f_ref[...] = -14.0 - lse_lead(parts_ref)
    columns_lse(f_ref, first_ref, rest_ref, quarter_ref[0], wide_ref, part_ref)
    send(part_ref, out_ref)


def last_columns_kernel(parts_ref, first_ref, rest_ref, quarter_ref, out_ref, f_ref, wide_ref, part_ref, row_ref):
    f = -14.0 - lse_lead(parts_ref)
    f_ref[...] = f
    columns_lse(f_ref, first_ref, rest_ref, quarter_ref[0], wide_ref, part_ref)
    for block in range(NB):
        row_ref[:, block * T : (block + 1) * T] = part_ref[block : block + 1, :]
    row_ref[:, SIDE : SIDE + T] = jnp.sum(f, axis=0, keepdims=True)
    send(row_ref, out_ref)


def finish_kernel(parts_ref, f_ref, quarter_ref, value_ref, potential_ref):
    total = tree(jnp.add, [parts_ref[k, :, SIDE : SIDE + T] for k in range(parts_ref.shape[0])])
    mean = jnp.sum(total) * (0.25 / 16384.0)
    value_ref[...] = (f_ref[pl.ds(quarter_ref[0] * 2, 2), :] - mean) * BACK
    for quarter in range(4):
        parts = [parts_ref[member(quarter, z, y), :, 0:SIDE] for z in range(4) for y in range(4)]
        top, whole = lse_list(parts)
        potential_ref[quarter] = (-15.0 - (top + jnp.log2(whole))) * BACK


SPEC = pl.BlockSpec(memory_space=pltpu.VMEM)
SCALARS = pl.BlockSpec(memory_space=pltpu.SMEM)
FAR = pl.BlockSpec(memory_space=pltpu.HBM)


def vmem(shape, dtype=F32):
    return pltpu.VMEM(shape, dtype)


def far(x):
    return pltpu.with_memory_space_constraint(x, pltpu.HBM)


def shape(dims, dtype=F32):
    return jax.ShapeDtypeStruct(dims, dtype)


def call(kernel, out, ins, scratch=()):
    return pl.pallas_call(
        kernel,
        out_shape=out,
        in_specs=ins,
        out_specs=[SPEC] * len(out),
        scratch_shapes=list(scratch),
        compiler_params=PARAMS,
    )


def local(pool, window_index, pool_labels, val_embed, val_labels, class_cost):
    quarter = lax.axis_index(QUAD).astype(jnp.int32).reshape(1)
    (columns,) = call(
        columns_kernel, [shape((64, 16, T))], [FAR], [vmem((2, 4096)), pltpu.SemaphoreType.DMA(())]
    )(far(val_embed.T))
    columns, window_index = lax.optimization_barrier((columns, window_index))
    (rows,) = call(
        rows_kernel,
        [shape((OWN + 8, T))],
        [FAR] * 3,
        [
            pltpu.SMEM(window_index.shape, jnp.int32),
            pltpu.SMEM(pool_labels.shape, jnp.int32),
            vmem(pool.shape),
            vmem((OWN, T)),
            pltpu.SemaphoreType.DMA((3,)),
        ],
    )(far(window_index), far(pool_labels), far(pool))
    columns = lax.all_to_all(columns, ROW, 0, 0, axis_index_groups=ROW_ORDER)
    others = {apart: lax.ppermute(rows, QUAD, [(i, i ^ apart) for i in range(4)]) for apart in (2, 3, 1)}
    rows, val_labels, class_cost = lax.optimization_barrier((rows, val_labels, class_cost))
    (kinds,) = call(labels_kernel, [shape((T, SIDE), BF16)], [SCALARS, SPEC, SPEC])(
        quarter, val_labels.reshape(32, T), class_cost
    )
    part, piece, wide = vmem((NB, T)), vmem((NB, T, T)), vmem((SIDE, T))
    (left,) = call(left_kernel, [shape((2 * OWN, 7 * T), BF16)], [SPEC] * 2)(rows, others[1])
    first, part_first, b = call(
        first_costs_kernel,
        [shape((2 * OWN, SIDE)), shape((NB, T)), shape((7 * T, SIDE), BF16)],
        [SPEC] * 3 + [SCALARS],
        [vmem((2, 2, T, T))],
    )(left, columns.reshape(SIDE, T), kinds, quarter)
    rest, parts = call(
        other_costs_kernel,
        [shape((2 * OWN, SIDE)), shape((32, NB, T))],
        [SPEC] * 3 + [SCALARS, SPEC],
        [part, vmem((2, 2, T, T))],
    )(others[2], others[3], b, quarter, part_first)
    step = [SPEC] * 3 + [SCALARS]
    parts = lax.all_to_all(parts, ALONG, 0, 0, axis_index_groups=ALONG_ORDER)
    (parts,) = call(columns_step_kernel, [shape((16, NB, T))], step, [wide, part, part])(parts, first, rest, quarter)
    parts = lax.all_to_all(parts, ACROSS, 0, 0, axis_index_groups=ACROSS_ORDER)
    (parts,) = call(rows_step_kernel, [shape((32, NB, T))], step, [piece, part])(parts, first, rest, quarter)
    parts = lax.all_to_all(parts, ALONG, 0, 0, axis_index_groups=ALONG_ORDER)
    parts, f = call(
        last_columns_kernel, [shape((64, 1, SIDE + T)), shape((NB, T))], step, [wide, part, vmem((1, SIDE + T))]
    )(parts, first, rest, quarter)
    parts = lax.all_to_all(parts, ROW, 0, 0, axis_index_groups=ROW_ORDER)
    value, potential = call(finish_kernel, [shape((2, T)), shape((4, 1, SIDE))], [SPEC, SPEC, SCALARS])(parts, f, quarter)
    return value.reshape(256), potential.reshape(4096)


def solution(mesh):
    fine = Mesh(mesh.devices.reshape(2, 2, 2, 2, 2, 2, 4, 2), ROW + COL)
    placed = (P(ROW, None), P(ROW), P(ROW), P(COL, ROW), P(COL), P())
    return jax.shard_map(local, mesh=fine, in_specs=placed, out_specs=(P(ROW), P(COL)), check_vma=False)
```

```python
import math

import jax
import jax.numpy as jnp
from jax import lax
from jax.experimental import pallas as pl
from jax.experimental.pallas import tpu as pltpu
from jax.sharding import Mesh
from jax.sharding import PartitionSpec as P

EPSILON = 0.02
SCALE = 1.0 / (EPSILON * math.log(2.0))
BACK = EPSILON * math.log(2.0)

ROW = ("z2", "z1", "z0", "y2", "y1", "y0")
COL = ("x", "core")
QUAD = ("z0", "y0")
ACROSS = ("z2", "z1", "y2", "y1")
ALONG = QUAD + COL

FIRST = (4, 4)


def turned(z_size, y_size, z_first, y_first):
    return [[(z + z_first) % z_size * y_size + (y + y_first) % y_size for z in range(z_size) for y in range(y_size)]]


ROW_ORDER = turned(8, 8, *FIRST)
ACROSS_ORDER = turned(4, 4, FIRST[0] // 2, FIRST[1] // 2)
ALONG_ORDER = [[(quarter ^ 3) * 8 + (x + 2) % 4 * 2 + (1 - core) for quarter in range(4) for x in range(4) for core in range(2)]]

T = 128
NB = 8
SIDE = NB * T
OWN = 256
PARAMS = pltpu.CompilerParams(vmem_limit_bytes=20 * 1024 * 1024)
F32 = jnp.float32
BF16 = jnp.bfloat16


def split3(x):
    hi = x.astype(BF16)
    rest = x - hi.astype(F32)
    mid = rest.astype(BF16)
    low = (rest - mid.astype(F32)).astype(BF16)
    return hi, mid, low


def member(quarter, z, y):
    return ((z * 2 + quarter // 2) * 4 + y) * 2 + quarter % 2


def in_order(y):
    places = [(z - FIRST[0]) % 8 * 2 + (half - FIRST[1] // 4) % 2 for z in range(8) for half in range(2)]
    return jnp.concatenate([y[8 * place : 8 * place + 8] for place in places], axis=0)


def tree(op, xs):
    xs = list(xs)
    while len(xs) > 1:
        xs = [op(*xs[i : i + 2]) if i + 1 < len(xs) else xs[i] for i in range(0, len(xs), 2)]
    return xs[0]


def lse_list(zs):
    top = tree(jnp.maximum, zs)
    return top, tree(jnp.add, [jnp.exp2(z - top) for z in zs])


def lse_lead(parts_ref):
    top, total = lse_list([parts_ref[k] for k in range(parts_ref.shape[0])])
    return top + jnp.log2(total)


def send(part_ref, out_ref):
    part = part_ref[...]
    for k in range(out_ref.shape[0]):
        out_ref[k] = part


def columns_kernel(val_hbm, columns_ref, val_ref, sem):
    copy = pltpu.make_async_copy(val_hbm, val_ref, sem)
    copy.start()
    copy.wait()
    for quarter in range(4):
        first = member(quarter, 0, 0)
        for block in range(NB):
            piece = val_ref[:, pl.ds((quarter * NB + block) * T, T)]
            for feature in range(2):
                columns_ref[first, pl.ds(feature * NB + block, 1), :] = piece[feature : feature + 1]
        whole = columns_ref[first]
        for z in range(4):
            for y in range(4):
                if z or y:
                    columns_ref[member(quarter, z, y)] = whole


def rows_kernel(index_hbm, labels_hbm, pool_hbm, rows_ref, index_ref, labels_ref, pool_ref, column_ref, sems):
    moves = [(index_hbm, index_ref), (labels_hbm, labels_ref), (pool_hbm, pool_ref)]
    copies = [pltpu.make_async_copy(a, b, sems.at[k]) for k, (a, b) in enumerate(moves)]
    for copy in copies:
        copy.start()
    for copy in copies:
        copy.wait()

    def step(i, carry):
        for j in range(16):
            at = i * 16 + j
            place = index_ref[at]
            rows_ref[pl.ds(at, 1), :] = pool_ref[pl.ds(place, 1), :]
            column_ref[pl.ds(at, 1), :] = jnp.full((1, T), labels_ref[place].astype(F32), F32)
        return carry

    lax.fori_loop(0, OWN // 16, step, 0)
    flat = [column_ref[k * T : (k + 1) * T, :].T[0:1] for k in range(OWN // T)]
    rows_ref[OWN : OWN + 8, :] = jnp.concatenate(flat + [jnp.zeros((8 - OWN // T, T), F32)], axis=0)


def labels_kernel(quarter_ref, labels_ref, class_ref, out_ref):
    classes = class_ref.shape[0]
    own = labels_ref[pl.ds(pl.multiple_of(quarter_ref[0] * NB, NB), NB), :]
    kinds = class_ref[...] * (-SCALE)
    for block in range(NB):
        onehot = (lax.broadcasted_iota(jnp.int32, (classes, T), 0) == own[block : block + 1]).astype(F32)
        mapped = jnp.dot(kinds, onehot, precision=lax.Precision.HIGHEST, preferred_element_type=F32)
        mapped = jnp.concatenate([mapped, jnp.zeros((16 - classes, T), F32)], axis=0)
        hi, mid, low = split3(mapped)
        filled = jnp.concatenate([hi, mid, low, jnp.zeros((T - 48, T), BF16)], axis=0)
        out_ref[:, block * T : (block + 1) * T] = filled


def rows_block(load, piece_ref):
    for piece in range(T // 32):
        top, total = lse_list([load(block, piece * 32) for block in range(NB)])
        piece_ref[piece * 32 : (piece + 1) * 32, :] = top + jnp.log2(total)
    flat = piece_ref[...].T
    top = jnp.max(flat, axis=0, keepdims=True)
    return top + jnp.log2(jnp.sum(jnp.exp2(flat - top), axis=0, keepdims=True))


def left_rows(rows_ref):
    x = rows_ref[0:OWN, :]
    squares = jnp.sum(x * x, axis=1, keepdims=True) * (-SCALE / T)
    hi, mid, low = split3(x * (2.0 * SCALE / T))
    lane = lax.broadcasted_iota(jnp.int32, (OWN, T), 1)
    flat = [jnp.broadcast_to(rows_ref[OWN + k : OWN + k + 1, :], (T, T)).T for k in range(OWN // T)]
    label = jnp.concatenate(flat, axis=0).astype(jnp.int32)
    ext = jnp.where((lane % 16 == label) & (lane < 48), 1.0, 0.0).astype(BF16)
    return jnp.concatenate([hi, hi, mid, hi, low, mid, ext], axis=1), squares


def group_costs(left, b, squares_v, cost_ref, start):
    a, squares = left
    cost_ref[start : start + OWN, :] = jnp.dot(a, b, preferred_element_type=F32) + squares + squares_v


def group_lse(cost_ref, start, place, part_ref, piece_ref):
    for half in range(OWN // T):

        def load(block, row):
            first = start + half * T + row
            return cost_ref[first : first + 32, block * T : (block + 1) * T]

        part_ref[pl.ds(place + half, 1), :] = rows_block(load, piece_ref.at[half])


def first_costs_kernel(rows_ref, rows3_ref, val_ref, kinds_ref, quarter_ref, cost_ref, part_ref, b_ref, squares_ref, piece_ref):
    for block in range(NB):
        lanes = slice(block * T, (block + 1) * T)
        y = in_order(val_ref[pl.ds(block, T, stride=NB), :])
        hi, mid, low = split3(y)
        for k, part in enumerate((hi, mid, hi, low, hi, mid)):
            b_ref[k * T : (k + 1) * T, lanes] = part
        squares_ref[:, lanes] = jnp.broadcast_to(jnp.sum(y * y, axis=0, keepdims=True) * (-SCALE / T), (8, T))
    b_ref[6 * T : 7 * T, :] = kinds_ref[...]
    tile_costs((rows_ref, rows3_ref), (0, 1), quarter_ref[0], b_ref, squares_ref, cost_ref, part_ref, piece_ref)


def other_costs_kernel(
    rows1_ref, rows2_ref, b_ref, squares_ref, quarter_ref, part_ref, cost_ref, out_ref, full_ref, piece_ref
):
    full_ref[...] = part_ref[...]
    tile_costs((rows1_ref, rows2_ref), (2, 3), quarter_ref[0], b_ref, squares_ref, cost_ref, full_ref, piece_ref)
    send(full_ref, out_ref)


def tile_costs(groups, aparts, quarter, b_ref, squares_ref, cost_ref, part_ref, piece_ref):
    for k, rows_ref in enumerate(groups):
        group_costs(left_rows(rows_ref), b_ref[...], squares_ref[0:1, :], cost_ref, k * OWN)
    for k, apart in enumerate(aparts):
        group_lse(cost_ref, k * OWN, (quarter ^ apart) * 2, part_ref, piece_ref.at[k])


def tile_rows(first_ref, rest_ref, s):
    return (first_ref, s * T) if s < NB // 2 else (rest_ref, (s - NB // 2) * T)


def place(quarter, s):
    return (quarter ^ (0, 1, 2, 3)[s // 2]) * 2 + s % 2


def rows_step_kernel(parts_ref, first_ref, rest_ref, quarter_ref, out_ref, piece_ref, part_ref):
    g = -15.0 - lse_lead(parts_ref)
    wide = [jnp.broadcast_to(g[block : block + 1], (32, T)) for block in range(NB)]
    for s in range(NB):
        cost_ref, start = tile_rows(first_ref, rest_ref, s)

        def load(block, row):
            return cost_ref[start + row : start + row + 32, block * T : (block + 1) * T] + wide[block]

        part_ref[pl.ds(place(quarter_ref[0], s), 1), :] = rows_block(load, piece_ref.at[s])
    send(part_ref, out_ref)


def columns_lse(f_ref, first_ref, rest_ref, quarter, wide_ref, part_ref):
    for s in range(NB):
        row = f_ref[pl.ds(place(quarter, s), 1), :]
        wide_ref[s * T : (s + 1) * T, :] = jnp.broadcast_to(row, (T, T)).T
    for block in range(NB):
        lanes = slice(block * T, (block + 1) * T)
        tops, totals = [], []
        for chunk in range(SIDE // 64):
            cost_ref, first = tile_rows(first_ref, rest_ref, chunk // 2)
            first = first + chunk % 2 * 64
            zs = []
            for j in range(0, 64, 8):
                at = chunk * 64 + j
                zs.append(cost_ref[first + j : first + j + 8, lanes] + wide_ref[at : at + 8, :])
            top, total = lse_list(zs)
            tops.append(top)
            totals.append(total)
        best = jnp.max(tree(jnp.maximum, tops), axis=0, keepdims=True)
        total = tree(jnp.add, [total * jnp.exp2(top - best) for top, total in zip(tops, totals)])
        part_ref[block : block + 1, :] = best + jnp.log2(jnp.sum(total, axis=0, keepdims=True))


def columns_step_kernel(parts_ref, first_ref, rest_ref, quarter_ref, out_ref, wide_ref, part_ref, f_ref):
    f_ref[...] = -14.0 - lse_lead(parts_ref)
    columns_lse(f_ref, first_ref, rest_ref, quarter_ref[0], wide_ref, part_ref)
    send(part_ref, out_ref)


def last_columns_kernel(parts_ref, first_ref, rest_ref, quarter_ref, out_ref, f_ref, wide_ref, part_ref, row_ref):
    f = -14.0 - lse_lead(parts_ref)
    f_ref[...] = f
    columns_lse(f_ref, first_ref, rest_ref, quarter_ref[0], wide_ref, part_ref)
    for block in range(NB):
        row_ref[:, block * T : (block + 1) * T] = part_ref[block : block + 1, :]
    row_ref[:, SIDE : SIDE + T] = jnp.sum(f, axis=0, keepdims=True)
    send(row_ref, out_ref)


def finish_kernel(parts_ref, f_ref, quarter_ref, value_ref, potential_ref):
    total = tree(jnp.add, [parts_ref[k, :, SIDE : SIDE + T] for k in range(parts_ref.shape[0])])
    mean = jnp.sum(total) * (0.25 / 16384.0)
    value_ref[...] = (f_ref[pl.ds(quarter_ref[0] * 2, 2), :] - mean) * BACK
    for quarter in range(4):
        parts = [parts_ref[member(quarter, z, y), :, 0:SIDE] for z in range(4) for y in range(4)]
        top, whole = lse_list(parts)
        potential_ref[quarter] = (-15.0 - (top + jnp.log2(whole))) * BACK


SPEC = pl.BlockSpec(memory_space=pltpu.VMEM)
SCALARS = pl.BlockSpec(memory_space=pltpu.SMEM)
FAR = pl.BlockSpec(memory_space=pltpu.HBM)


def vmem(shape, dtype=F32):
    return pltpu.VMEM(shape, dtype)


def far(x):
    return pltpu.with_memory_space_constraint(x, pltpu.HBM)


def shape(dims, dtype=F32):
    return jax.ShapeDtypeStruct(dims, dtype)


def call(kernel, out, ins, scratch=()):
    return pl.pallas_call(
        kernel,
        out_shape=out,
        in_specs=ins,
        out_specs=[SPEC] * len(out),
        scratch_shapes=list(scratch),
        compiler_params=PARAMS,
    )


def local(pool, window_index, pool_labels, val_embed, val_labels, class_cost):
    quarter = lax.axis_index(QUAD).astype(jnp.int32).reshape(1)
    (columns,) = call(
        columns_kernel, [shape((64, 16, T))], [FAR], [vmem((2, 4096)), pltpu.SemaphoreType.DMA(())]
    )(far(val_embed.T))
    columns, window_index = lax.optimization_barrier((columns, window_index))
    (rows,) = call(
        rows_kernel,
        [shape((OWN + 8, T))],
        [FAR] * 3,
        [
            pltpu.SMEM(window_index.shape, jnp.int32),
            pltpu.SMEM(pool_labels.shape, jnp.int32),
            vmem(pool.shape),
            vmem((OWN, T)),
            pltpu.SemaphoreType.DMA((3,)),
        ],
    )(far(window_index), far(pool_labels), far(pool))
    columns = lax.all_to_all(columns, ROW, 0, 0, axis_index_groups=ROW_ORDER)
    others = {apart: lax.ppermute(rows, QUAD, [(i, i ^ apart) for i in range(4)]) for apart in (2, 3, 1)}
    rows, val_labels, class_cost = lax.optimization_barrier((rows, val_labels, class_cost))
    (kinds,) = call(labels_kernel, [shape((T, SIDE), BF16)], [SCALARS, SPEC, SPEC])(
        quarter, val_labels.reshape(32, T), class_cost
    )
    part, piece, wide = vmem((NB, T)), vmem((NB, T, T)), vmem((SIDE, T))
    first, part_first, b, squares = call(
        first_costs_kernel,
        [shape((2 * OWN, SIDE)), shape((NB, T)), shape((7 * T, SIDE), BF16), shape((8, SIDE))],
        [SPEC] * 4 + [SCALARS],
        [vmem((2, 2, T, T))],
    )(rows, others[1], columns.reshape(SIDE, T), kinds, quarter)
    rest, parts = call(
        other_costs_kernel,
        [shape((2 * OWN, SIDE)), shape((32, NB, T))],
        [SPEC] * 4 + [SCALARS, SPEC],
        [part, vmem((2, 2, T, T))],
    )(others[2], others[3], b, squares, quarter, part_first)
    step = [SPEC] * 3 + [SCALARS]
    parts = lax.all_to_all(parts, ALONG, 0, 0, axis_index_groups=ALONG_ORDER)
    (parts,) = call(columns_step_kernel, [shape((16, NB, T))], step, [wide, part, part])(parts, first, rest, quarter)
    parts = lax.all_to_all(parts, ACROSS, 0, 0, axis_index_groups=ACROSS_ORDER)
    (parts,) = call(rows_step_kernel, [shape((32, NB, T))], step, [piece, part])(parts, first, rest, quarter)
    parts = lax.all_to_all(parts, ALONG, 0, 0, axis_index_groups=ALONG_ORDER)
    parts, f = call(
        last_columns_kernel, [shape((64, 1, SIDE + T)), shape((NB, T))], step, [wide, part, vmem((1, SIDE + T))]
    )(parts, first, rest, quarter)
    parts = lax.all_to_all(parts, ROW, 0, 0, axis_index_groups=ROW_ORDER)
    value, potential = call(finish_kernel, [shape((2, T)), shape((4, 1, SIDE))], [SPEC, SPEC, SCALARS])(parts, f, quarter)
    return value.reshape(256), potential.reshape(4096)


def solution(mesh):
    fine = Mesh(mesh.devices.reshape(2, 2, 2, 2, 2, 2, 4, 2), ROW + COL)
    placed = (P(ROW, None), P(ROW), P(ROW), P(COL, ROW), P(COL), P())
    return jax.shard_map(local, mesh=fine, in_specs=placed, out_specs=(P(ROW), P(COL)), check_vma=False)
```
